32 devices in a mesh: inp: 4 (over z), out: 2 (over y), tok: 4 (over x, core).
Axes of the slice: x: 2, y: 2, z: 4, core: 2. Of those that a mesh axis runs over, the one named last changes fastest.
Arguments:
- saved_input: float32 [512, 4096], P('tok', 'inp'), may hold values from -6 to 6
- saved_gate: float32 [512, 28672], P('inp', ('out', 'tok')), may hold values from -6 to 6
- saved_up: float32 [512, 28672], P('inp', ('out', 'tok')), may hold values from -6 to 6
- out_grad: bfloat16 [512, 4096], P('tok', 'inp'), may hold values from -1.5 to 1.5
- w_gate: bfloat16 [4096, 28672], P('inp', ('out', 'tok')), may hold values from -0.09375 to 0.09375
- w_up: bfloat16 [4096, 28672], P('inp', ('out', 'tok')), may hold values from -0.09375 to 0.09375
- w_down: bfloat16 [28672, 4096], P(('out', 'tok'), 'inp'), may hold values from -0.03125 to 0.03125
Outputs:
- input_grad: bfloat16 [512, 4096], P(('out', 'tok'), 'inp')
- gate_wgrad: bfloat16 [4096, 28672], P('inp', ('out', 'tok'))
- up_wgrad: bfloat16 [4096, 28672], P('inp', ('out', 'tok'))
- down_wgrad: bfloat16 [28672, 4096], P(('out', 'tok'), 'inp')
The draws below stay inside these ranges and needn't reach their ends.
All inputs are finite; a program needn't handle non-finite values.
Results may differ from the reference program's by a relative error of at most 0.0057.
Values may be sent and summed in bfloat16 or wider, within the bound.
No kernel may reach another device: no remote copies, remote signals or barrier semaphores. Data moves between devices by JAX's collectives and lax.ppermute only.
A program may use at most 128 MiB of HBM per device.

```python
import jax
import jax.numpy as jnp

D = 4096
FF = 28672
TOKENS = 512


def block_levels(own_key, shape, cuts, least, top_value):
    factor_of, own = 1.0, jax.random.fold_in(own_key, 6)
    for axis_at, blocks in cuts:
        steps = jnp.exp(jax.random.uniform(jax.random.fold_in(own, axis_at), (blocks,), jnp.float32, least / len(cuts), top_value / len(cuts)))
        factor_of = factor_of * jnp.repeat(steps, shape[axis_at] // blocks).reshape([-1 if axis == axis_at else 1 for axis in range(len(shape))])
    return factor_of


def bell_draw(key, shape, scale, bound, pieces=(), kind=jnp.bfloat16):
    level = block_levels(key, shape, pieces, -0.22, 0.18) if pieces else 1.0
    array = jax.random.normal(key, shape, jnp.float32) * scale * level
    return jnp.minimum(jnp.maximum(array, -bound), bound).astype(kind)


def setup_inputs(seed: int = 0) -> dict:
    streams_of = jax.random.split(jax.random.key(seed), 8)
    saved_input = bell_draw(streams_of[0], (TOKENS, D), 1.0, 6.0, ((0, 4), (1, 4)), jnp.float32)
    saved_gate = bell_draw(streams_of[1], (TOKENS, FF), 1.0, 6.0, ((0, 4), (1, 8)), jnp.float32)
    saved_up = bell_draw(streams_of[2], (TOKENS, FF), 1.0, 6.0, ((0, 4), (1, 8)), jnp.float32)
    out_grad = bell_draw(streams_of[3], (TOKENS, D), 0.25, 1.5, ((0, 4), (1, 4)))
    w_gate = bell_draw(streams_of[4], (D, FF), D ** -0.5, 0.09375, ((0, 4), (1, 8)))
    w_up = bell_draw(streams_of[5], (D, FF), D ** -0.5, 0.09375, ((0, 4), (1, 8)))
    w_down = bell_draw(streams_of[6], (FF, D), FF ** -0.5, 0.03125, ((0, 8), (1, 4)))
    return {"saved_input": saved_input, "saved_gate": saved_gate, "saved_up": saved_up, "out_grad": out_grad, "w_gate": w_gate, "w_up": w_up, "w_down": w_down}


def reference(saved_input, saved_gate, saved_up, out_grad, w_gate, w_up, w_down):
    input_b = saved_input.astype(jnp.bfloat16)
    hidden_grad = jnp.dot(out_grad, w_down.T, preferred_element_type=jnp.float32)
    sig = jax.nn.sigmoid(saved_gate)
    hidden = (saved_gate * sig * saved_up).astype(jnp.bfloat16)
    gate_grad = (hidden_grad * saved_up * sig * (1.0 + saved_gate * (1.0 - sig))).astype(jnp.bfloat16)
    up_grad = (hidden_grad * saved_gate * sig).astype(jnp.bfloat16)
    gate_wgrad = jnp.dot(input_b.T, gate_grad, preferred_element_type=jnp.float32).astype(jnp.bfloat16)
    up_wgrad = jnp.dot(input_b.T, up_grad, preferred_element_type=jnp.float32).astype(jnp.bfloat16)
    down_wgrad = jnp.dot(hidden.T, out_grad, preferred_element_type=jnp.float32).astype(jnp.bfloat16)
    total = jnp.dot(gate_grad, w_gate.T, preferred_element_type=jnp.float32)
    total = total + jnp.dot(up_grad, w_up.T, preferred_element_type=jnp.float32)
    input_grad = total.astype(jnp.bfloat16)
    return input_grad, gate_wgrad, up_wgrad, down_wgrad
```

```python
import functools

import jax
import jax.numpy as jnp
from jax import lax
from jax.experimental import pallas as pl
from jax.experimental.pallas import tpu as pltpu
from jax.sharding import PartitionSpec as P

BF, F32 = jnp.bfloat16, jnp.float32
LAST = (((1,), (1,)), ((), ()))
LEAD = (((0,), (0,)), ((), ()))
STRAIGHT = (((1,), (0,)), ((), ()))
ANY = pl.BlockSpec(memory_space=pl.ANY)
VMEM_LIMIT = 64 * 1024 * 1024

ENDS_IN = [(0, 1), (3, 2)]
MIDDLE = [(1, 2), (2, 1)]
PAIRS = [(0, 1), (1, 0), (2, 3), (3, 2)]
OUTWARD = [(1, 0), (2, 3)]
X_SWAP = [(0, 2), (2, 0), (1, 3), (3, 1)]
CORE_SWAP = [(0, 1), (1, 0), (2, 3), (3, 2)]
Y_SWAP = [(0, 1), (1, 0)]
XY_SWAP = [(4 * o + t, 4 * (1 - o) + (t ^ 2)) for o in range(2) for t in range(4)]


def send(x, perm):
    return lax.ppermute(x, "inp", perm)


def place(k, z):
    return jnp.where(k // 2 == z // 2, k ^ z, jnp.where(z < 2, k, 3 - k))


def dot(a, b, dims):
    return lax.dot_general(a, b, dims, preferred_element_type=F32)


class Chain:
    def __init__(self, token):
        self.token = token

    def call(self, body, grid, ins, in_specs, outs, out_specs, aliases=(), scalars=None, scratch=()):
        lead = 0 if scalars is None else 1

        def kernel(*refs):
            body(*refs[:lead], *refs[lead + 1 : lead + 1 + len(ins)], *refs[lead + 2 + len(ins) :])

        pairs = {lead: 0, **{lead + 1 + i: 1 + o for i, o in aliases}}
        given = pl.pallas_call(
            kernel,
            grid_spec=pltpu.PrefetchScalarGridSpec(
                num_scalar_prefetch=lead,
                grid=grid,
                in_specs=[ANY, *in_specs],
                out_specs=[ANY, *out_specs],
                scratch_shapes=list(scratch),
            ),
            out_shape=[jax.ShapeDtypeStruct(self.token.shape, self.token.dtype), *outs],
            input_output_aliases=pairs,
            compiler_params=pltpu.CompilerParams(vmem_limit_bytes=VMEM_LIMIT),
        )(*(() if scalars is None else (scalars,)), self.token, *ins)
        self.token = given[0]
        return given[1:]

    def relay(self, *arrays):
        return self.call(
            lambda *refs: None,
            (1,),
            arrays,
            [ANY] * len(arrays),
            [jax.ShapeDtypeStruct(a.shape, a.dtype) for a in arrays],
            [ANY] * len(arrays),
            aliases=[(i, i) for i in range(len(arrays))],
        )


TILE = 256
CUTS = (7, 7)


def swiglu_grads(part_ref, second_ref, third_ref, g_ref, u_ref, out_ref):
    share = part_ref[...] + third_ref[...].astype(F32) + second_ref[...].astype(F32)
    g, u = g_ref[...], u_ref[...]
    sig = jax.nn.sigmoid(g)
    out_ref[0] = (share * u * sig * (1.0 + g * (1.0 - sig))).astype(BF)
    out_ref[1] = (share * g * sig).astype(BF)


def add_part(got_ref, part_ref, out_ref):
    out_ref[...] = (got_ref[...].astype(F32) + part_ref[...]).astype(BF)


def add_parts(second_ref, part_ref, first_ref, next_ref, third_ref, pass_ref):
    add_part(second_ref, part_ref, third_ref)
    add_part(first_ref, next_ref, pass_ref)


def partial_sums(grads_ref, w_ref, part_ref, rest_ref):
    part = dot(grads_ref[...], w_ref[...], LAST)
    part_ref[...] = part
    rest_ref[...] = part[part.shape[0] // 2 :].astype(BF)


def arrange(turn, where_ref, *refs):
    out_ref, rows = refs[4], refs[0].shape[0]
    for r, block in enumerate(refs[:4]):
        at = pl.multiple_of(place(r ^ where_ref[2], where_ref[0]) * rows, rows)
        if turn:
            out_ref[:, pl.ds(at, rows)] = block[...].T
        else:
            out_ref[pl.ds(at, rows), :] = block[...]


def first_partial_sums(where_ref, *refs):
    blocks, w_ref, part_ref, rest_ref, grads_ref = refs[:4], *refs[4:]

    @pl.when(pl.program_id(0) == 0)
    def _():
        arrange(False, where_ref, *blocks, grads_ref)

    partial_sums(grads_ref, w_ref, part_ref, rest_ref)


def hidden_values(g_ref, u_ref, out_ref):
    g = g_ref[...]
    out_ref[...] = (g * jax.nn.sigmoid(g) * u_ref[...]).astype(BF)


def joined(own, pair, near, near_end, far, far_end):
    return jnp.concatenate([own, pair, near + near_end, far + far_end], axis=0)


def input_sums(piece_refs, held, wg_ref, wu_ref):
    @pl.when(pl.program_id(0) == 0)
    def _():
        for which in range(2):
            held[which] = joined(*[r[which] for r in piece_refs])

    return dot(held[0], wg_ref[...], LAST) + dot(held[1], wu_ref[...], LAST)


def input_sums_first(*refs):
    refs[8][...] = input_sums(refs[:6], refs[9], *refs[6:8])


def input_sums_last(where_ref, *refs):
    mine_ref, other_ref, held, total = refs[9:]
    total[...] = refs[8][...] + input_sums(refs[:6], held, *refs[6:8])
    half = total.shape[0] // 8
    z, core = where_ref[0], where_ref[2] % 2
    for k in range(4):
        start = place(k, z) * 2
        rows = slice(k * half, (k + 1) * half)
        mine_ref[rows, :] = total[pl.ds(pl.multiple_of((start + core) * half, half), half), :]
        other_ref[rows, :] = total[pl.ds(pl.multiple_of((start + 1 - core) * half, half), half), :].astype(BF)


def weight_grads(inputs_ref, *refs):
    gate_ref, up_ref = refs[-2:]
    gate_ref[...] = dot(inputs_ref[...], joined(*[r[0] for r in refs[:6]]), STRAIGHT).astype(BF)
    up_ref[...] = dot(inputs_ref[...], joined(*[r[1] for r in refs[:6]]), STRAIGHT).astype(BF)


def down_grads(grads_ref, *refs):
    own, pair, pair_end, *rest = [r[...] for r in refs[:7]]
    refs[-1][...] = dot(joined(own, pair + pair_end, *rest), grads_ref[...], LEAD).astype(BF)


def split_again(where_ref, mine_ref, got_ref, keep_ref, y_ref, x_ref, xy_ref):
    rows = keep_ref.shape[0]
    o, half = where_ref[1], where_ref[2] // 2

    def summed(to_o, to_half):
        at = pl.ds(pl.multiple_of((2 * to_o + to_half) * rows, rows), rows)
        return mine_ref[at, :] + got_ref[at, :].astype(F32)

    keep_ref[...] = summed(o, half)
    y_ref[...] = summed(1 - o, half).astype(BF)
    x_ref[...] = summed(o, 1 - half).astype(BF)
    xy_ref[...] = summed(1 - o, 1 - half).astype(BF)


def add_last(keep_ref, y_ref, x_ref, xy_ref, out_ref):
    total = keep_ref[...] + y_ref[...].astype(F32) + x_ref[...].astype(F32) + xy_ref[...].astype(F32)
    out_ref[...] = total.astype(BF)


def shape(dims, dtype):
    return jax.ShapeDtypeStruct(dims, dtype)


def line_of_four(saved_input, saved_gate, saved_up, out_grad, w_gate, w_up, w_down):
    rows, ff = saved_gate.shape
    depth = w_gate.shape[0]
    tokens = 4 * rows
    z, o, t = lax.axis_index("inp"), lax.axis_index("out"), lax.axis_index("tok")
    where = jnp.stack([z, o, t]).astype(jnp.int32)
    chain = Chain(jnp.zeros((8, 128), F32))
    step = ff // 14
    widths = [c * step for c in CUTS]
    cuts = [(sum(widths[:c]), w) for c, w in enumerate(widths)]

    def cols(height, tile, start, row=0):
        return pl.BlockSpec((height, tile), lambda j, *_: (row, start // tile + j))

    def whole(*dims):
        return pl.BlockSpec(dims, lambda *_: (0,) * len(dims))

    def gathered(x):
        other = lax.ppermute(x, "tok", X_SWAP)
        return x, lax.ppermute(x, "tok", CORE_SWAP), other, lax.ppermute(other, "tok", CORE_SWAP)

    def hidden_of():
        tile = ff // 7
        return chain.call(
            hidden_values,
            (7,),
            (saved_gate, saved_up),
            [cols(rows, tile, 0)] * 2,
            [shape((rows, ff), BF)],
            [cols(rows, tile, 0)],
        )[0]

    def partial(c):
        start, w = cuts[c]
        tile = TILE
        w_spec = pl.BlockSpec((tile, depth), lambda j, *_: (start // tile + j, 0))
        outs = [shape((tokens, w), F32), shape((tokens // 2, w), BF)]
        specs = [cols(tokens, tile, 0), cols(tokens // 2, tile, 0)]
        if c:
            part, rest = chain.call(
                partial_sums, (w // tile,), (grads, w_down), [whole(tokens, depth), w_spec], outs, specs
            )
            given = grads
        else:
            part, rest, given = chain.call(
                first_partial_sums,
                (w // tile,),
                (*gathered(out_grad), w_down),
                [whole(rows, depth)] * 4 + [w_spec],
                [*outs, shape((tokens, depth), BF)],
                [*specs, whole(tokens, depth)],
                scalars=where,
            )
        return given, part, send(rest, ENDS_IN)

    def pass_on(c):
        w = widths[c]
        tile = TILE
        second = chain.call(
            add_part,
            (w // tile,),
            (firsts[c], parts[c]),
            [cols(2 * rows, tile, 0), cols(2 * rows, tile, 0, 1)],
            [shape((2 * rows, w), BF)],
            [cols(2 * rows, tile, 0)],
        )[0]
        seconds[c] = send(second, MIDDLE)

    def hand_out(c):
        w = widths[c]
        third_in = [cols(rows, w, 0, 1)] * 2
        if c + 1 == len(cuts):
            third = chain.call(
                add_part, (1,), (seconds[c], parts[c]), third_in, [shape((rows, w), BF)], [whole(rows, w)]
            )[0]
        else:
            v = widths[c + 1]
            third, second = chain.call(
                add_parts,
                (1,),
                (seconds[c], parts[c], firsts[c + 1], parts[c + 1]),
                [*third_in, whole(2 * rows, v), cols(2 * rows, v, 0, 1)],
                [shape((rows, w), BF), shape((2 * rows, v), BF)],
                [whole(rows, w), whole(2 * rows, v)],
            )
            seconds[c + 1] = send(second, MIDDLE)
        thirds[c] = send(third, PAIRS)

    def grads_of(c):
        start, w = cuts[c]
        tile = TILE
        own = chain.call(
            swiglu_grads,
            (w // tile,),
            (parts[c], seconds[c], thirds[c], saved_gate, saved_up),
            [cols(rows, tile, 0)] * 3 + [cols(rows, tile, start)] * 2,
            [shape((2, rows, w), BF)],
            [pl.BlockSpec((2, rows, tile), lambda j: (0, 0, j))],
        )[0]
        return spread(own)

    def spread(own):
        return {"own": own, "pair": send(own, PAIRS), "near": send(own, MIDDLE)}

    def spread_far(x, *others):
        x["pair"], x["near"], *others = chain.relay(x["pair"], x["near"], *others)
        x["near_end"] = send(x["near"], OUTWARD)
        x["far"] = send(x["pair"], MIDDLE)
        return others

    def spread_end(x, *others):
        x["far"], *others = chain.relay(x["far"], *others)
        x["far_end"] = send(x["far"], OUTWARD)
        return others

    def pieces(x):
        return [x[k] for k in ("own", "pair", "near", "near_end", "far", "far_end")]

    def input_step(c, before):
        start, w = cuts[c]
        tile = TILE
        first, last = before is None, c + 1 == len(cuts)
        wide = pl.BlockSpec((pl.Element(tile), pl.Element(w)), lambda j, *_: (j * tile, start))
        across = cols(tokens, tile, 0)
        held = [pltpu.VMEM((2, tokens, w), BF)]
        ins = [*pieces(groups[c]), w_gate, w_up]
        specs = [whole(2, rows, w)] * 6 + [wide, wide]
        if first:
            return chain.call(
                input_sums_first, (depth // tile,), ins, specs, [shape((tokens, depth), F32)], [across], scratch=held
            )[0]
        return chain.call(
            input_sums_last,
            (depth // tile,),
            [*ins, before],
            [*specs, across],
            [shape((tokens // 2, depth), F32), shape((tokens // 2, depth), BF)],
            [cols(tokens // 2, tile, 0)] * 2,
            scalars=where,
            scratch=[*held, pltpu.VMEM((tokens, tile), F32)],
        )

    def weights_step(c, before):
        start, w = cuts[c]
        tile = TILE
        return chain.call(
            weight_grads,
            (w // tile,),
            (inputs, *pieces(groups[c]), *before),
            [whole(depth, tokens)] + [pl.BlockSpec((2, rows, tile), lambda j: (0, 0, j))] * 6 + [ANY] * len(before),
            [shape((depth, ff), BF)] * 2,
            [cols(depth, tile, start)] * 2,
            aliases=[(7, 0), (8, 1)] if before else (),
        )

    def down_step():
        tile = TILE
        return chain.call(
            down_grads,
            (ff // tile,),
            [grads, *[h[k] for k in ("own", "pair", "pair_end", "near", "near_end", "far", "far_end")]],
            [whole(tokens, depth)] + [cols(rows, tile, 0)] * 7,
            [shape((ff, depth), BF)],
            [pl.BlockSpec((tile, depth), lambda j, *_: (j, 0))],
        )[0]

    n = len(cuts)
    parts, firsts, seconds, thirds, groups = ([None] * n for _ in range(5))
    h = {"own": hidden_of()}
    h["pair_end"] = send(h["own"], OUTWARD)
    h["near"] = send(h["own"], MIDDLE)
    grads, parts[0], firsts[0] = partial(0)
    _, parts[1], firsts[1] = partial(1)
    h["near"], h["pair_end"], h_again = chain.relay(h["near"], h["pair_end"], h["own"])
    h["near_end"] = send(h["near"], OUTWARD)
    pass_on(0)
    hand_out(0)
    (h["near_end"],) = chain.relay(h["near_end"])
    groups[0] = grads_of(0)
    hand_out(1)
    h_again, = spread_far(groups[0], h_again)
    h["pair"] = send(h_again, ENDS_IN)
    groups[1] = grads_of(1)
    (inputs_b,) = spread_end(groups[0], saved_input.astype(BF))
    inputs = chain.call(
        functools.partial(arrange, True),
        (1,),
        gathered(inputs_b),
        [whole(rows, depth)] * 4,
        [shape((depth, tokens), BF)],
        [whole(depth, tokens)],
        scalars=where,
    )[0]
    (h["pair"],) = chain.relay(h["pair"])
    h["far"] = send(h["pair"], MIDDLE)
    (groups[0]["near_end"],) = spread_far(groups[1], groups[0]["near_end"])
    h["far"], groups[0]["far_end"] = spread_end(groups[1], h["far"], groups[0]["far_end"])
    h["far_end"] = send(h["far"], OUTWARD)
    total = input_step(0, None)
    weights = weights_step(0, ())
    mine, other = input_step(1, total)
    got = lax.ppermute(other, "tok", CORE_SWAP)
    keep, *others = chain.call(
        split_again,
        (1,),
        (mine, got),
        [whole(tokens // 2, depth)] * 2,
        [shape((rows // 2, depth), F32), *[shape((rows // 2, depth), BF)] * 3],
        [whole(rows // 2, depth)] * 4,
        scalars=where,
    )
    got = (
        lax.ppermute(others[2], ("out", "tok"), XY_SWAP),
        lax.ppermute(others[0], "out", Y_SWAP),
        lax.ppermute(others[1], "tok", X_SWAP),
    )
    weights = weights_step(1, weights)
    result = chain.call(
        add_last,
        (1,),
        (keep, got[1], got[2], got[0]),
        [whole(rows // 2, depth)] * 4,
        [shape((rows // 2, depth), BF)],
        [whole(rows // 2, depth)],
    )[0]
    down = down_step()
    return result, weights[0], weights[1], down


def any_line(saved_input, saved_gate, saved_up, out_grad, w_gate, w_up, w_down):
    inputs = lax.all_gather(saved_input.astype(BF), "tok", axis=0, tiled=True)
    grads = lax.all_gather(out_grad, "tok", axis=0, tiled=True)
    part = dot(grads, w_down, LAST)
    share = lax.psum_scatter(part, "inp", scatter_dimension=0, tiled=True)
    sig = jax.nn.sigmoid(saved_gate)
    gate = share * saved_up * sig * (1.0 + saved_gate * (1.0 - sig))
    up = share * saved_gate * sig
    hidden = saved_gate * sig * saved_up
    gate, up, hidden = (
        lax.all_gather(v.astype(BF), "inp", axis=0, tiled=True) for v in (gate, up, hidden)
    )
    total = dot(gate, w_gate, LAST) + dot(up, w_up, LAST)
    total = lax.psum_scatter(total, ("out", "tok"), scatter_dimension=0, tiled=True)
    return (
        total.astype(BF),
        dot(inputs, gate, LEAD).astype(BF),
        dot(inputs, up, LEAD).astype(BF),
        dot(hidden, grads, LEAD).astype(BF),
    )


def solution(mesh):
    sizes = dict(mesh.shape)
    placed = (
        P("tok", "inp"),
        P("inp", ("out", "tok")),
        P("inp", ("out", "tok")),
        P("tok", "inp"),
        P("inp", ("out", "tok")),
        P("inp", ("out", "tok")),
        P(("out", "tok"), "inp"),
    )

    def local(*args):
        rows, ff = args[1].shape
        fits = (sizes["inp"], sizes["out"], sizes["tok"]) == (4, 2, 4)
        if fits and rows % 32 == 0 and ff % 3584 == 0:
            return line_of_four(*args)
        return any_line(*args)

    return jax.shard_map(
        local,
        mesh=mesh,
        in_specs=placed,
        out_specs=(
            P(("out", "tok"), "inp"),
            P("inp", ("out", "tok")),
            P("inp", ("out", "tok")),
            P(("out", "tok"), "inp"),
        ),
        check_vma=False,
    )
```

```python
import functools

import jax
import jax.numpy as jnp
from jax import lax
from jax.experimental import pallas as pl
from jax.experimental.pallas import tpu as pltpu
from jax.sharding import PartitionSpec as P

BF, F32 = jnp.bfloat16, jnp.float32
LAST = (((1,), (1,)), ((), ()))
LEAD = (((0,), (0,)), ((), ()))
STRAIGHT = (((1,), (0,)), ((), ()))
ANY = pl.BlockSpec(memory_space=pl.ANY)
VMEM_LIMIT = 64 * 1024 * 1024

ENDS_IN = [(0, 1), (3, 2)]
MIDDLE = [(1, 2), (2, 1)]
PAIRS = [(0, 1), (1, 0), (2, 3), (3, 2)]
OUTWARD = [(1, 0), (2, 3)]
X_SWAP = [(0, 2), (2, 0), (1, 3), (3, 1)]
CORE_SWAP = [(0, 1), (1, 0), (2, 3), (3, 2)]
Y_SWAP = [(0, 1), (1, 0)]
XY_SWAP = [(4 * o + t, 4 * (1 - o) + (t ^ 2)) for o in range(2) for t in range(4)]


def send(x, perm):
    return lax.ppermute(x, "inp", perm)


def tile_of(size, most):
    return max(t for t in range(128, most + 1, 128) if size % t == 0)


def place(k, z):
    return jnp.where(k // 2 == z // 2, k ^ z, jnp.where(z < 2, k, 3 - k))


def dot(a, b, dims):
    return lax.dot_general(a, b, dims, preferred_element_type=F32)


class Chain:
    def __init__(self, token):
        self.token = token

    def call(self, body, grid, ins, in_specs, outs, out_specs, aliases=(), scalars=None, scratch=()):
        lead = 0 if scalars is None else 1

        def kernel(*refs):
            body(*refs[:lead], *refs[lead + 1 : lead + 1 + len(ins)], *refs[lead + 2 + len(ins) :])

        pairs = {lead: 0, **{lead + 1 + i: 1 + o for i, o in aliases}}
        given = pl.pallas_call(
            kernel,
            grid_spec=pltpu.PrefetchScalarGridSpec(
                num_scalar_prefetch=lead,
                grid=grid,
                in_specs=[ANY, *in_specs],
                out_specs=[ANY, *out_specs],
                scratch_shapes=list(scratch),
            ),
            out_shape=[jax.ShapeDtypeStruct(self.token.shape, self.token.dtype), *outs],
            input_output_aliases=pairs,
            compiler_params=pltpu.CompilerParams(vmem_limit_bytes=VMEM_LIMIT),
        )(*(() if scalars is None else (scalars,)), self.token, *ins)
        self.token = given[0]
        return given[1:]

    def relay(self, *arrays):
        return self.call(
            lambda *refs: None,
            (1,),
            arrays,
            [ANY] * len(arrays),
            [jax.ShapeDtypeStruct(a.shape, a.dtype) for a in arrays],
            [ANY] * len(arrays),
            aliases=[(i, i) for i in range(len(arrays))],
        )


CUTS = (7, 7)


def swiglu_grads(part_ref, second_ref, third_ref, g_ref, u_ref, out_ref):
    share = part_ref[...] + third_ref[...].astype(F32) + second_ref[...].astype(F32)
    g, u = g_ref[...], u_ref[...]
    sig = jax.nn.sigmoid(g)
    out_ref[0] = (share * u * sig * (1.0 + g * (1.0 - sig))).astype(BF)
    out_ref[1] = (share * g * sig).astype(BF)


def add_part(got_ref, part_ref, out_ref):
    out_ref[...] = (got_ref[...].astype(F32) + part_ref[...]).astype(BF)


def add_parts(second_ref, part_ref, first_ref, next_ref, third_ref, pass_ref):
    add_part(second_ref, part_ref, third_ref)
    add_part(first_ref, next_ref, pass_ref)


def partial_sums(grads_ref, w_ref, part_ref, rest_ref):
    part = dot(grads_ref[...], w_ref[...], LAST)
    part_ref[...] = part
    rest_ref[...] = part[part.shape[0] // 2 :].astype(BF)


def arrange(turn, where_ref, *refs):
    out_ref, rows = refs[4], refs[0].shape[0]
    for r, block in enumerate(refs[:4]):
        at = pl.multiple_of(place(r ^ where_ref[2], where_ref[0]) * rows, rows)
        if turn:
            out_ref[:, pl.ds(at, rows)] = block[...].T
        else:
            out_ref[pl.ds(at, rows), :] = block[...]


def first_partial_sums(where_ref, *refs):
    blocks, w_ref, part_ref, rest_ref, grads_ref = refs[:4], *refs[4:]

    @pl.when(pl.program_id(0) == 0)
    def _():
        arrange(False, where_ref, *blocks, grads_ref)

    partial_sums(grads_ref, w_ref, part_ref, rest_ref)


def hidden_values(g_ref, u_ref, out_ref):
    g = g_ref[...]
    out_ref[...] = (g * jax.nn.sigmoid(g) * u_ref[...]).astype(BF)


def joined(own, pair, near, near_end, far, far_end):
    return jnp.concatenate([own, pair, near + near_end, far + far_end], axis=0)


def input_sums(piece_refs, held, wg_ref, wu_ref):
    @pl.when(pl.program_id(0) == 0)
    def _():
        for which in range(2):
            held[which] = joined(*[r[which] for r in piece_refs])

    return dot(held[0], wg_ref[...], LAST) + dot(held[1], wu_ref[...], LAST)


def input_sums_first(*refs):
    refs[8][...] = input_sums(refs[:6], refs[9], *refs[6:8])


def input_sums_last(where_ref, *refs):
    mine_ref, other_ref, held, total = refs[9:]
    total[...] = refs[8][...] + input_sums(refs[:6], held, *refs[6:8])
    half = total.shape[0] // 8
    z, core = where_ref[0], where_ref[2] % 2
    for k in range(4):
        start = place(k, z) * 2
        rows = slice(k * half, (k + 1) * half)
        mine_ref[rows, :] = total[pl.ds(pl.multiple_of((start + core) * half, half), half), :]
        other_ref[rows, :] = total[pl.ds(pl.multiple_of((start + 1 - core) * half, half), half), :].astype(BF)


def weight_grads(inputs_ref, *refs):
    gate_ref, up_ref = refs[-2:]
    gate_ref[...] = dot(inputs_ref[...], joined(*[r[0] for r in refs[:6]]), STRAIGHT).astype(BF)
    up_ref[...] = dot(inputs_ref[...], joined(*[r[1] for r in refs[:6]]), STRAIGHT).astype(BF)


def down_grads(grads_ref, *refs):
    refs[-1][...] = dot(joined(*[r[...] for r in refs[:6]]), grads_ref[...], LEAD).astype(BF)


def split_again(where_ref, mine_ref, got_ref, keep_ref, y_ref, x_ref, xy_ref):
    rows = keep_ref.shape[0]
    o, half = where_ref[1], where_ref[2] // 2

    def summed(to_o, to_half):
        at = pl.ds(pl.multiple_of((2 * to_o + to_half) * rows, rows), rows)
        return mine_ref[at, :] + got_ref[at, :].astype(F32)

    keep_ref[...] = summed(o, half)
    y_ref[...] = summed(1 - o, half).astype(BF)
    x_ref[...] = summed(o, 1 - half).astype(BF)
    xy_ref[...] = summed(1 - o, 1 - half).astype(BF)


def add_last(keep_ref, y_ref, x_ref, xy_ref, out_ref):
    total = keep_ref[...] + y_ref[...].astype(F32) + x_ref[...].astype(F32) + xy_ref[...].astype(F32)
    out_ref[...] = total.astype(BF)


def shape(dims, dtype):
    return jax.ShapeDtypeStruct(dims, dtype)


def line_of_four(saved_input, saved_gate, saved_up, out_grad, w_gate, w_up, w_down):
    rows, ff = saved_gate.shape
    depth = w_gate.shape[0]
    tokens = 4 * rows
    z, o, t = lax.axis_index("inp"), lax.axis_index("out"), lax.axis_index("tok")
    where = jnp.stack([z, o, t]).astype(jnp.int32)
    chain = Chain(jnp.zeros((8, 128), F32))
    step = ff // 14
    widths = [c * step for c in CUTS]
    cuts = [(sum(widths[:c]), w) for c, w in enumerate(widths)]

    def cols(height, tile, start, row=0):
        return pl.BlockSpec((height, tile), lambda j, *_: (row, start // tile + j))

    def whole(*dims):
        return pl.BlockSpec(dims, lambda *_: (0,) * len(dims))

    def tok_swaps(x):
        return x, lax.ppermute(x, "tok", CORE_SWAP), lax.ppermute(x, "tok", X_SWAP)

    def tok_last(x, sibling, other):
        (other,) = chain.relay(other)
        return x, sibling, other, lax.ppermute(other, "tok", CORE_SWAP)

    def hidden_args():
        tile = tile_of(ff, 2048)
        return (
            hidden_values,
            (ff // tile,),
            (saved_gate, saved_up),
            [cols(rows, tile, 0)] * 2,
            [shape((rows, ff), BF)],
            [cols(rows, tile, 0)],
        )

    def partial(c):
        start, w = cuts[c]
        tile = tile_of(w, 1024)
        w_spec = pl.BlockSpec((tile, depth), lambda j, *_: (start // tile + j, 0))
        outs = [shape((tokens, w), F32), shape((tokens // 2, w), BF)]
        specs = [cols(tokens, tile, 0), cols(tokens // 2, tile, 0)]
        if c:
            part, rest = chain.call(
                partial_sums, (w // tile,), (grads, w_down), [whole(tokens, depth), w_spec], outs, specs
            )
            given = grads
        else:
            part, rest, given = chain.call(
                first_partial_sums,
                (w // tile,),
                (*out_grads, w_down),
                [whole(rows, depth)] * 4 + [w_spec],
                [*outs, shape((tokens, depth), BF)],
                [*specs, whole(tokens, depth)],
                scalars=where,
            )
        return given, part, send(rest, ENDS_IN)

    def pass_on(c):
        w = widths[c]
        tile = tile_of(w, 1024)
        second = chain.call(
            add_part,
            (w // tile,),
            (firsts[c], parts[c]),
            [cols(2 * rows, tile, 0), cols(2 * rows, tile, 0, 1)],
            [shape((2 * rows, w), BF)],
            [cols(2 * rows, tile, 0)],
        )[0]
        seconds[c] = send(second, MIDDLE)

    def hand_out(c):
        w = widths[c]
        third_in = [cols(rows, w, 0, 1)] * 2
        if c + 1 == len(cuts):
            third = chain.call(
                add_part, (1,), (seconds[c], parts[c]), third_in, [shape((rows, w), BF)], [whole(rows, w)]
            )[0]
        else:
            v = widths[c + 1]
            third, second = chain.call(
                add_parts,
                (1,),
                (seconds[c], parts[c], firsts[c + 1], parts[c + 1]),
                [*third_in, whole(2 * rows, v), cols(2 * rows, v, 0, 1)],
                [shape((rows, w), BF), shape((2 * rows, v), BF)],
                [whole(rows, w), whole(2 * rows, v)],
            )
            seconds[c + 1] = send(second, MIDDLE)
        thirds[c] = send(third, PAIRS)

    def grads_of(c):
        start, w = cuts[c]
        tile = tile_of(w, 1024)
        own = chain.call(
            swiglu_grads,
            (w // tile,),
            (parts[c], seconds[c], thirds[c], saved_gate, saved_up),
            [cols(rows, tile, 0)] * 3 + [cols(rows, tile, start)] * 2,
            [shape((2, rows, w), BF)],
            [pl.BlockSpec((2, rows, tile), lambda j: (0, 0, j))],
        )[0]
        return spread(own)

    def spread(own):
        return {"own": own, "pair": send(own, PAIRS), "near": send(own, MIDDLE)}

    def spread_near(x):
        (x["near"],) = chain.relay(x["near"])
        x["near_end"] = send(x["near"], OUTWARD)

    def spread_far(x):
        (x["pair"],) = chain.relay(x["pair"])
        x["far"] = send(x["pair"], MIDDLE)

    def spread_end(x, *others):
        x["far"], *others = chain.relay(x["far"], *others)
        x["far_end"] = send(x["far"], OUTWARD)
        return others

    def pieces(x):
        return [x[k] for k in ("own", "pair", "near", "near_end", "far", "far_end")]

    def input_step(c, before):
        start, w = cuts[c]
        tile = tile_of(depth, 512)
        first, last = before is None, c + 1 == len(cuts)
        wide = pl.BlockSpec((pl.Element(tile), pl.Element(w)), lambda j, *_: (j * tile, start))
        across = cols(tokens, tile, 0)
        held = [pltpu.VMEM((2, tokens, w), BF)]
        ins = [*pieces(groups[c]), w_gate, w_up]
        specs = [whole(2, rows, w)] * 6 + [wide, wide]
        if first:
            return chain.call(
                input_sums_first, (depth // tile,), ins, specs, [shape((tokens, depth), F32)], [across], scratch=held
            )[0]
        return chain.call(
            input_sums_last,
            (depth // tile,),
            [*ins, before],
            [*specs, across],
            [shape((tokens // 2, depth), F32), shape((tokens // 2, depth), BF)],
            [cols(tokens // 2, tile, 0)] * 2,
            scalars=where,
            scratch=[*held, pltpu.VMEM((tokens, tile), F32)],
        )

    def weights_step(c, before):
        start, w = cuts[c]
        tile = tile_of(w, 1024)
        return chain.call(
            weight_grads,
            (w // tile,),
            (inputs, *pieces(groups[c]), *before),
            [whole(depth, tokens)] + [pl.BlockSpec((2, rows, tile), lambda j: (0, 0, j))] * 6 + [ANY] * len(before),
            [shape((depth, ff), BF)] * 2,
            [cols(depth, tile, start)] * 2,
            aliases=[(7, 0), (8, 1)] if before else (),
        )

    def down_step():
        tile = tile_of(ff, 1024)
        return chain.call(
            down_grads,
            (ff // tile,),
            [grads, *pieces(h)],
            [whole(tokens, depth)] + [cols(rows, tile, 0)] * 6,
            [shape((ff, depth), BF)],
            [pl.BlockSpec((tile, depth), lambda j, *_: (j, 0))],
        )[0]

    n = len(cuts)
    parts, firsts, seconds, thirds, groups = ([None] * n for _ in range(5))
    out_grads = tok_swaps(out_grad)
    h = spread(Chain(jnp.zeros((8, 128), F32)).call(*hidden_args())[0])
    out_grads = tok_last(*out_grads)
    grads, parts[0], firsts[0] = partial(0)
    _, parts[1], firsts[1] = partial(1)
    spread_near(h)
    spread_far(h)
    pass_on(0)
    (h["near_end"],) = spread_end(h, h["near_end"])
    hand_out(0)
    (h["far_end"],) = chain.relay(h["far_end"])
    groups[0] = grads_of(0)
    hand_out(1)
    spread_far(groups[0])
    (thirds[1],) = chain.relay(thirds[1])
    spread_near(groups[0])
    groups[1] = grads_of(1)
    spread_end(groups[0])
    (groups[0]["near_end"],) = chain.relay(groups[0]["near_end"])
    (inputs_b,) = chain.relay(saved_input.astype(BF))
    in_raw = tok_last(*tok_swaps(inputs_b))
    inputs = chain.call(
        functools.partial(arrange, True),
        (1,),
        in_raw,
        [whole(rows, depth)] * 4,
        [shape((depth, tokens), BF)],
        [whole(depth, tokens)],
        scalars=where,
    )[0]
    down = down_step()
    spread_near(groups[1])
    spread_far(groups[1])
    (groups[0]["far_end"],) = chain.relay(groups[0]["far_end"])
    total = input_step(0, None)
    weights = weights_step(0, ())
    spread_end(groups[1])
    mine, other = input_step(1, total)
    got = lax.ppermute(other, "tok", CORE_SWAP)
    keep, *others = chain.call(
        split_again,
        (1,),
        (mine, got),
        [whole(tokens // 2, depth)] * 2,
        [shape((rows // 2, depth), F32), *[shape((rows // 2, depth), BF)] * 3],
        [whole(rows // 2, depth)] * 4,
        scalars=where,
    )
    got = (
        lax.ppermute(others[2], ("out", "tok"), XY_SWAP),
        lax.ppermute(others[0], "out", Y_SWAP),
        lax.ppermute(others[1], "tok", X_SWAP),
    )
    weights = weights_step(1, weights)
    result = chain.call(
        add_last,
        (1,),
        (keep, got[1], got[2], got[0]),
        [whole(rows // 2, depth)] * 4,
        [shape((rows // 2, depth), BF)],
        [whole(rows // 2, depth)],
    )[0]
    return result, weights[0], weights[1], down


def any_line(saved_input, saved_gate, saved_up, out_grad, w_gate, w_up, w_down):
    inputs = lax.all_gather(saved_input.astype(BF), "tok", axis=0, tiled=True)
    grads = lax.all_gather(out_grad, "tok", axis=0, tiled=True)
    part = dot(grads, w_down, LAST)
    share = lax.psum_scatter(part, "inp", scatter_dimension=0, tiled=True)
    sig = jax.nn.sigmoid(saved_gate)
    gate = share * saved_up * sig * (1.0 + saved_gate * (1.0 - sig))
    up = share * saved_gate * sig
    hidden = saved_gate * sig * saved_up
    gate, up, hidden = (
        lax.all_gather(v.astype(BF), "inp", axis=0, tiled=True) for v in (gate, up, hidden)
    )
    total = dot(gate, w_gate, LAST) + dot(up, w_up, LAST)
    total = lax.psum_scatter(total, ("out", "tok"), scatter_dimension=0, tiled=True)
    return (
        total.astype(BF),
        dot(inputs, gate, LEAD).astype(BF),
        dot(inputs, up, LEAD).astype(BF),
        dot(hidden, grads, LEAD).astype(BF),
    )


def solution(mesh):
    sizes = dict(mesh.shape)
    placed = (
        P("tok", "inp"),
        P("inp", ("out", "tok")),
        P("inp", ("out", "tok")),
        P("tok", "inp"),
        P("inp", ("out", "tok")),
        P("inp", ("out", "tok")),
        P(("out", "tok"), "inp"),
    )

    def local(*args):
        rows, ff = args[1].shape
        fits = (sizes["inp"], sizes["out"], sizes["tok"]) == (4, 2, 4)
        if fits and rows % 32 == 0 and ff % 3584 == 0:
            return line_of_four(*args)
        return any_line(*args)

    return jax.shard_map(
        local,
        mesh=mesh,
        in_specs=placed,
        out_specs=(
            P(("out", "tok"), "inp"),
            P("inp", ("out", "tok")),
            P("inp", ("out", "tok")),
            P(("out", "tok"), "inp"),
        ),
        check_vma=False,
    )
```

```python
import functools

import jax
import jax.numpy as jnp
from jax import lax
from jax.experimental import pallas as pl
from jax.experimental.pallas import tpu as pltpu
from jax.sharding import PartitionSpec as P

BF, F32 = jnp.bfloat16, jnp.float32
LAST = (((1,), (1,)), ((), ()))
LEAD = (((0,), (0,)), ((), ()))
STRAIGHT = (((1,), (0,)), ((), ()))
ANY = pl.BlockSpec(memory_space=pl.ANY)
MIB = 1024 * 1024
SMALL, MEDIUM, LARGE = 8, 16, 28

ENDS_IN = [(0, 1), (3, 2)]
MIDDLE = [(1, 2), (2, 1)]
PAIRS = [(0, 1), (1, 0), (2, 3), (3, 2)]
OUTWARD = [(1, 0), (2, 3)]
X_SWAP = [(0, 2), (2, 0), (1, 3), (3, 1)]
CORE_SWAP = [(0, 1), (1, 0), (2, 3), (3, 2)]
Y_SWAP = [(0, 1), (1, 0)]
XY_SWAP = [(4 * o + t, 4 * (1 - o) + (t ^ 2)) for o in range(2) for t in range(4)]


def send(x, perm):
    return lax.ppermute(x, "inp", perm)


LAST_TILE = 512
ALL = ("own", "pair", "near", "near_end", "far", "far_end")


def tile_of(size, most):
    return max(t for t in range(128, most + 1, 128) if size % t == 0)


def place(k, z):
    return jnp.where(k // 2 == z // 2, k ^ z, jnp.where(z < 2, k, 3 - k))


def dot(a, b, dims):
    return lax.dot_general(a, b, dims, preferred_element_type=F32)


class Chain:
    def __init__(self, token):
        self.token = token

    def call(self, body, grid, ins, in_specs, outs, out_specs, aliases=(), scalars=None, scratch=(), mib=SMALL):
        lead = 0 if scalars is None else 1

        def kernel(*refs):
            body(*refs[:lead], *refs[lead + 1 : lead + 1 + len(ins)], *refs[lead + 2 + len(ins) :])

        pairs = {lead: 0, **{lead + 1 + i: 1 + o for i, o in aliases}}
        given = pl.pallas_call(
            kernel,
            grid_spec=pltpu.PrefetchScalarGridSpec(
                num_scalar_prefetch=lead,
                grid=grid,
                in_specs=[ANY, *in_specs],
                out_specs=[ANY, *out_specs],
                scratch_shapes=list(scratch),
            ),
            out_shape=[jax.ShapeDtypeStruct(self.token.shape, self.token.dtype), *outs],
            input_output_aliases=pairs,
            compiler_params=pltpu.CompilerParams(vmem_limit_bytes=mib * MIB),
        )(*(() if scalars is None else (scalars,)), self.token, *ins)
        self.token = given[0]
        return given[1:]

    def relay(self, *arrays):
        return self.call(
            lambda *refs: None,
            (1,),
            arrays,
            [ANY] * len(arrays),
            [jax.ShapeDtypeStruct(a.shape, a.dtype) for a in arrays],
            [ANY] * len(arrays),
            aliases=[(i, i) for i in range(len(arrays))],
        )


def swiglu_grads(part_ref, second_ref, third_ref, g_ref, u_ref, out_ref):
    share = part_ref[...] + third_ref[...].astype(F32) + second_ref[...].astype(F32)
    g, u = g_ref[...], u_ref[...]
    sig = jax.nn.sigmoid(g)
    out_ref[0] = (share * u * sig * (1.0 + g * (1.0 - sig))).astype(BF)
    out_ref[1] = (share * g * sig).astype(BF)


def add_part(got_ref, part_ref, out_ref):
    out_ref[...] = (got_ref[...].astype(F32) + part_ref[...]).astype(BF)


def add_parts(second_ref, part_ref, first_ref, next_ref, third_ref, pass_ref):
    add_part(second_ref, part_ref, third_ref)
    add_part(first_ref, next_ref, pass_ref)


def partial_sums(grads_ref, w_ref, part_ref, rest_ref):
    part = dot(grads_ref[...], w_ref[...], LAST)
    part_ref[...] = part
    rest_ref[...] = part[part.shape[0] // 2 :].astype(BF)


def arrange(turn, where_ref, *refs):
    out_ref, rows = refs[4], refs[0].shape[0]
    for r, block in enumerate(refs[:4]):
        at = pl.multiple_of(place(r ^ where_ref[2], where_ref[0]) * rows, rows)
        if turn:
            out_ref[:, pl.ds(at, rows)] = block[...].T
        else:
            out_ref[pl.ds(at, rows), :] = block[...]


def first_partial_sums(where_ref, *refs):
    blocks, w_ref, part_ref, rest_ref, grads_ref = refs[:4], *refs[4:]

    @pl.when(pl.program_id(0) == 0)
    def _():
        arrange(False, where_ref, *blocks, grads_ref)

    partial_sums(grads_ref, w_ref, part_ref, rest_ref)


def hidden_values(g_ref, u_ref, out_ref):
    g = g_ref[...]
    out_ref[...] = (g * jax.nn.sigmoid(g) * u_ref[...]).astype(BF)


def joined(*pieces):
    alone = pieces[: len(pieces) % 4] if len(pieces) < 4 else pieces[:2]
    if len(pieces) == 2:
        alone = ()
    pairs = pieces[len(alone) :]
    return jnp.concatenate([*alone, *[a + b for a, b in zip(pairs[::2], pairs[1::2])]], axis=0)


def input_sums(piece_refs, held, wg_ref, wu_ref, before_ref):
    @pl.when(pl.program_id(0) == 0)
    def _():
        for which in range(2):
            held[which] = joined(*[r[which] for r in piece_refs])

    total = dot(held[0], wg_ref[...], LAST) + dot(held[1], wu_ref[...], LAST)
    return total if before_ref is None else total + before_ref[...]


def input_sums_first(count, *refs):
    refs[-2][...] = input_sums(refs[:count], refs[-1], *refs[count : count + 2], None)


def input_sums_more(count, *refs):
    refs[-2][...] = input_sums(refs[:count], refs[-1], *refs[count : count + 3])


def input_sums_last(where_ref, far_ref, end_ref, wg_ref, wu_ref, before_ref, others_ref, mine_ref, other_ref, held, total):
    rows = before_ref.shape[0]
    total[: 3 * rows, :] = others_ref[...]
    total[3 * rows :, :] = input_sums((far_ref, end_ref), held, wg_ref, wu_ref, before_ref)
    half = rows // 2
    z, core = where_ref[0], where_ref[2] % 2
    for k in range(4):
        start = place(k, z) * 2
        at = slice(k * half, (k + 1) * half)
        mine_ref[at, :] = total[pl.ds(pl.multiple_of((start + core) * half, half), half), :]
        other_ref[at, :] = total[pl.ds(pl.multiple_of((start + 1 - core) * half, half), half), :].astype(BF)


def weight_grads(inputs_ref, *refs):
    gate_ref, up_ref = refs[-2:]
    gate_ref[...] = dot(inputs_ref[...], joined(*[r[0] for r in refs[:6]]), STRAIGHT).astype(BF)
    up_ref[...] = dot(inputs_ref[...], joined(*[r[1] for r in refs[:6]]), STRAIGHT).astype(BF)


def down_grads(grads_ref, *refs):
    refs[-1][...] = dot(joined(*[r[...] for r in refs[:6]]), grads_ref[...], LEAD).astype(BF)


def split_again(where_ref, mine_ref, got_ref, keep_ref, y_ref, x_ref, xy_ref):
    rows = keep_ref.shape[0]
    o, half = where_ref[1], where_ref[2] // 2

    def summed(to_o, to_half):
        at = pl.ds(pl.multiple_of((2 * to_o + to_half) * rows, rows), rows)
        return mine_ref[at, :] + got_ref[at, :].astype(F32)

    keep_ref[...] = summed(o, half)
    y_ref[...] = summed(1 - o, half).astype(BF)
    x_ref[...] = summed(o, 1 - half).astype(BF)
    xy_ref[...] = summed(1 - o, 1 - half).astype(BF)


def add_last(keep_ref, y_ref, x_ref, xy_ref, out_ref):
    total = keep_ref[...] + y_ref[...].astype(F32) + x_ref[...].astype(F32) + xy_ref[...].astype(F32)
    out_ref[...] = total.astype(BF)


def shape(dims, dtype):
    return jax.ShapeDtypeStruct(dims, dtype)


def line_of_four(saved_input, saved_gate, saved_up, out_grad, w_gate, w_up, w_down):
    rows, ff = saved_gate.shape
    depth = w_gate.shape[0]
    tokens = 4 * rows
    z, o, t = lax.axis_index("inp"), lax.axis_index("out"), lax.axis_index("tok")
    where = jnp.stack([z, o, t]).astype(jnp.int32)
    chain = Chain(jnp.zeros((8, 128), F32))
    half = ff // 2
    cuts = [(0, half), (half, half)]
    widths = [half, half]
    group_cuts = cuts

    def cols(height, tile, start, row=0):
        return pl.BlockSpec((height, tile), lambda j, *_: (row, start // tile + j))

    def whole(*dims):
        return pl.BlockSpec(dims, lambda *_: (0,) * len(dims))

    def tok_swaps(x):
        return x, lax.ppermute(x, "tok", CORE_SWAP), lax.ppermute(x, "tok", X_SWAP)

    def tok_last(x, sibling, other):
        (other,) = chain.relay(other)
        return x, sibling, other, lax.ppermute(other, "tok", CORE_SWAP)

    def hidden_args():
        tile = tile_of(ff, 2048)
        return (
            hidden_values,
            (ff // tile,),
            (saved_gate, saved_up),
            [cols(rows, tile, 0)] * 2,
            [shape((rows, ff), BF)],
            [cols(rows, tile, 0)],
        )

    def partial(c):
        start, w = cuts[c]
        tile = tile_of(w, 1024)
        w_spec = pl.BlockSpec((tile, depth), lambda j, *_: (start // tile + j, 0))
        outs = [shape((tokens, w), F32), shape((tokens // 2, w), BF)]
        specs = [cols(tokens, tile, 0), cols(tokens // 2, tile, 0)]
        if c:
            part, rest = chain.call(
                partial_sums, (w // tile,), (grads, w_down), [whole(tokens, depth), w_spec], outs, specs, mib=MEDIUM)
            given = grads
        else:
            part, rest, given = chain.call(
                first_partial_sums,
                (w // tile,),
                (*out_grads, w_down),
                [whole(rows, depth)] * 4 + [w_spec],
                [*outs, shape((tokens, depth), BF)],
                [*specs, whole(tokens, depth)],
                scalars=where, mib=MEDIUM)
        return given, part, send(rest, ENDS_IN)

    def pass_on(c):
        w = widths[c]
        tile = tile_of(w, 1024)
        second = chain.call(
            add_part,
            (w // tile,),
            (firsts[c], parts[c]),
            [cols(2 * rows, tile, 0), cols(2 * rows, tile, 0, 1)],
            [shape((2 * rows, w), BF)],
            [cols(2 * rows, tile, 0)],
        )[0]
        seconds[c] = send(second, MIDDLE)

    def hand_out(c):
        w = widths[c]
        third_in = [cols(rows, w, 0, 1)] * 2
        if c + 1 == len(cuts):
            third = chain.call(
                add_part, (1,), (seconds[c], parts[c]), third_in, [shape((rows, w), BF)], [whole(rows, w)]
            )[0]
        else:
            v = widths[c + 1]
            third, second = chain.call(
                add_parts,
                (1,),
                (seconds[c], parts[c], firsts[c + 1], parts[c + 1]),
                [*third_in, whole(2 * rows, v), cols(2 * rows, v, 0, 1)],
                [shape((rows, w), BF), shape((2 * rows, v), BF)],
                [whole(rows, w), whole(2 * rows, v)],
            )
            seconds[c + 1] = send(second, MIDDLE)
        thirds[c] = send(third, PAIRS)

    def grads_of(c, g):
        start, w = group_cuts[g]
        tile = tile_of(w, 1024)
        at = start - cuts[c][0]
        own = chain.call(
            swiglu_grads,
            (w // tile,),
            (parts[c], seconds[c], thirds[c], saved_gate, saved_up),
            [cols(rows, tile, at)] * 3 + [cols(rows, tile, start)] * 2,
            [shape((2, rows, w), BF)],
            [pl.BlockSpec((2, rows, tile), lambda j: (0, 0, j))],
        )[0]
        return spread(own)

    def spread(own):
        return {"own": own, "pair": send(own, PAIRS), "near": send(own, MIDDLE)}

    def spread_near(x):
        (x["near"],) = chain.relay(x["near"])
        x["near_end"] = send(x["near"], OUTWARD)

    def spread_far(x):
        (x["pair"],) = chain.relay(x["pair"])
        x["far"] = send(x["pair"], MIDDLE)

    def spread_end(x, *others):
        x["far"], *others = chain.relay(x["far"], *others)
        x["far_end"] = send(x["far"], OUTWARD)
        return others

    def pieces(x):
        return [x[k] for k in ALL]

    def input_step(g, before, names):
        start, w = group_cuts[g]
        tile = tile_of(depth, 512)
        wide = pl.BlockSpec((pl.Element(tile), pl.Element(w)), lambda j: (j * tile, start))
        count = len(names)
        height = rows * len([k for k in names if not k.endswith("_end")])
        across = cols(height, tile, 0)
        return chain.call(
            functools.partial(input_sums_first if before is None else input_sums_more, count),
            (depth // tile,),
            [*[groups[g][k] for k in names], w_gate, w_up] + ([] if before is None else [before]),
            [whole(2, rows, w)] * count + [wide, wide] + ([] if before is None else [across]),
            [shape((height, depth), F32)],
            [across],
            scratch=[pltpu.VMEM((2, height, w), BF)], mib=LARGE)[0]

    def input_last(g, before, others):
        start, w = group_cuts[g]
        tile = tile_of(depth, LAST_TILE)
        wide = pl.BlockSpec((pl.Element(tile), pl.Element(w)), lambda j, *_: (j * tile, start))
        return chain.call(
            input_sums_last,
            (depth // tile,),
            [groups[g]["far"], groups[g]["far_end"], w_gate, w_up, before, others],
            [whole(2, rows, w)] * 2 + [wide, wide, cols(rows, tile, 0, 3), cols(3 * rows, tile, 0)],
            [shape((tokens // 2, depth), F32), shape((tokens // 2, depth), BF)],
            [cols(tokens // 2, tile, 0)] * 2,
            scalars=where,
            scratch=[pltpu.VMEM((2, rows, w), BF), pltpu.VMEM((tokens, tile), F32)], mib=LARGE)

    def weights_step(g, before):
        start, w = group_cuts[g]
        tile = tile_of(w, 1024)
        return chain.call(
            weight_grads,
            (w // tile,),
            (inputs, *pieces(groups[g]), *before),
            [whole(depth, tokens)] + [pl.BlockSpec((2, rows, tile), lambda j: (0, 0, j))] * 6 + [ANY] * len(before),
            [shape((depth, ff), BF)] * 2,
            [cols(depth, tile, start)] * 2,
            aliases=[(7, 0), (8, 1)] if before else (), mib=LARGE)

    def down_step():
        tile = tile_of(ff, 1024)
        return chain.call(
            down_grads,
            (ff // tile,),
            [grads, *pieces(h)],
            [whole(tokens, depth)] + [cols(rows, tile, 0)] * 6,
            [shape((ff, depth), BF)],
            [pl.BlockSpec((tile, depth), lambda j, *_: (j, 0))], mib=MEDIUM)[0]

    n = len(cuts)
    parts, firsts, seconds, thirds = ([None] * n for _ in range(4))
    out_grads = tok_swaps(out_grad)
    h = spread(Chain(jnp.zeros((8, 128), F32)).call(*hidden_args(), mib=MEDIUM)[0])
    out_grads = tok_last(*out_grads)
    grads, parts[0], firsts[0] = partial(0)
    _, parts[1], firsts[1] = partial(1)
    spread_near(h)
    spread_far(h)
    pass_on(0)
    (h["near_end"],) = spread_end(h, h["near_end"])
    hand_out(0)
    (h["far_end"],) = chain.relay(h["far_end"])
    groups = [grads_of(0, 0)]
    down = down_step()
    hand_out(1)
    spread_far(groups[0])
    (thirds[1],) = chain.relay(thirds[1])
    spread_near(groups[0])
    groups.append(grads_of(1, 1))
    spread_end(groups[0])
    (groups[0]["near_end"],) = chain.relay(groups[0]["near_end"])
    (inputs_b,) = chain.relay(saved_input.astype(BF))
    in_raw = tok_last(*tok_swaps(inputs_b))
    inputs = chain.call(
        functools.partial(arrange, True),
        (1,),
        in_raw,
        [whole(rows, depth)] * 4,
        [shape((depth, tokens), BF)],
        [whole(depth, tokens)],
        scalars=where,
    )[0]
    spread_near(groups[1])
    spread_far(groups[1])
    (groups[0]["far_end"],) = chain.relay(groups[0]["far_end"])
    total = input_step(0, None, ALL)
    weights = weights_step(0, ())
    spread_end(groups[1])
    others = input_step(1, total, ALL[:4])
    mine, other = input_last(1, total, others)
    got = lax.ppermute(other, "tok", CORE_SWAP)
    keep, *others = chain.call(
        split_again,
        (1,),
        (mine, got),
        [whole(tokens // 2, depth)] * 2,
        [shape((rows // 2, depth), F32), *[shape((rows // 2, depth), BF)] * 3],
        [whole(rows // 2, depth)] * 4,
        scalars=where,
    )
    got = (
        lax.ppermute(others[2], ("out", "tok"), XY_SWAP),
        lax.ppermute(others[0], "out", Y_SWAP),
        lax.ppermute(others[1], "tok", X_SWAP),
    )
    weights = weights_step(1, weights)
    result = chain.call(
        add_last,
        (1,),
        (keep, got[1], got[2], got[0]),
        [whole(rows // 2, depth)] * 4,
        [shape((rows // 2, depth), BF)],
        [whole(rows // 2, depth)],
    )[0]
    return result, weights[0], weights[1], down


def any_line(saved_input, saved_gate, saved_up, out_grad, w_gate, w_up, w_down):
    inputs = lax.all_gather(saved_input.astype(BF), "tok", axis=0, tiled=True)
    grads = lax.all_gather(out_grad, "tok", axis=0, tiled=True)
    part = dot(grads, w_down, LAST)
    share = lax.psum_scatter(part, "inp", scatter_dimension=0, tiled=True)
    sig = jax.nn.sigmoid(saved_gate)
    gate = share * saved_up * sig * (1.0 + saved_gate * (1.0 - sig))
    up = share * saved_gate * sig
    hidden = saved_gate * sig * saved_up
    gate, up, hidden = (
        lax.all_gather(v.astype(BF), "inp", axis=0, tiled=True) for v in (gate, up, hidden)
    )
    total = dot(gate, w_gate, LAST) + dot(up, w_up, LAST)
    total = lax.psum_scatter(total, ("out", "tok"), scatter_dimension=0, tiled=True)
    return (
        total.astype(BF),
        dot(inputs, gate, LEAD).astype(BF),
        dot(inputs, up, LEAD).astype(BF),
        dot(hidden, grads, LEAD).astype(BF),
    )


def solution(mesh):
    sizes = dict(mesh.shape)
    placed = (
        P("tok", "inp"),
        P("inp", ("out", "tok")),
        P("inp", ("out", "tok")),
        P("tok", "inp"),
        P("inp", ("out", "tok")),
        P("inp", ("out", "tok")),
        P(("out", "tok"), "inp"),
    )

    def local(*args):
        rows, ff = args[1].shape
        fits = (sizes["inp"], sizes["out"], sizes["tok"]) == (4, 2, 4)
        if fits and rows % 32 == 0 and ff % 3584 == 0:
            return line_of_four(*args)
        return any_line(*args)

    return jax.shard_map(
        local,
        mesh=mesh,
        in_specs=placed,
        out_specs=(
            P(("out", "tok"), "inp"),
            P("inp", ("out", "tok")),
            P("inp", ("out", "tok")),
            P(("out", "tok"), "inp"),
        ),
        check_vma=False,
    )
```

```python
import functools
import math

import jax
import jax.numpy as jnp
from jax import lax
from jax.experimental import pallas as pl
from jax.experimental.pallas import tpu as pltpu
from jax.sharding import PartitionSpec as P

BF, F32 = jnp.bfloat16, jnp.float32
LAST = (((1,), (1,)), ((), ()))
LEAD = (((0,), (0,)), ((), ()))
STRAIGHT = (((1,), (0,)), ((), ()))
ANY = pl.BlockSpec(memory_space=pl.ANY)
MIB = 1024 * 1024
SMALL, MEDIUM, LARGE, WHOLE = 8, 16, 28, 62

ENDS_IN = [(0, 1), (3, 2)]
MIDDLE = [(1, 2), (2, 1)]
PAIRS = [(0, 1), (1, 0), (2, 3), (3, 2)]
OUTWARD = [(1, 0), (2, 3)]
X_SWAP = [(0, 2), (2, 0), (1, 3), (3, 1)]
CORE_SWAP = [(0, 1), (1, 0), (2, 3), (3, 2)]
Y_SWAP = [(0, 1), (1, 0)]
XY_SWAP = [(4 * o + t, 4 * (1 - o) + (t ^ 2)) for o in range(2) for t in range(4)]


def send(x, perm):
    return lax.ppermute(x, "inp", perm)


LAST_TILE = 512
FIRST = 7
ALL = ("own", "pair", "near", "near_end", "far", "far_end")


def tile_of(size, most):
    return max(t for t in range(128, most + 1, 128) if size % t == 0)


def place(k, z):
    return jnp.where(k // 2 == z // 2, k ^ z, jnp.where(z < 2, k, 3 - k))


def dot(a, b, dims):
    return lax.dot_general(a, b, dims, preferred_element_type=F32)


class Chain:
    def __init__(self, token):
        self.token = token

    def call(self, body, grid, ins, in_specs, outs, out_specs, aliases=(), scalars=None, scratch=(), mib=SMALL):
        lead = 0 if scalars is None else 1

        def kernel(*refs):
            body(*refs[:lead], *refs[lead + 1 : lead + 1 + len(ins)], *refs[lead + 2 + len(ins) :])

        pairs = {lead: 0, **{lead + 1 + i: 1 + o for i, o in aliases}}
        given = pl.pallas_call(
            kernel,
            grid_spec=pltpu.PrefetchScalarGridSpec(
                num_scalar_prefetch=lead,
                grid=grid,
                in_specs=[ANY, *in_specs],
                out_specs=[ANY, *out_specs],
                scratch_shapes=list(scratch),
            ),
            out_shape=[jax.ShapeDtypeStruct(self.token.shape, self.token.dtype), *outs],
            input_output_aliases=pairs,
            compiler_params=pltpu.CompilerParams(vmem_limit_bytes=mib * MIB),
        )(*(() if scalars is None else (scalars,)), self.token, *ins)
        self.token = given[0]
        return given[1:]

    def relay(self, *arrays):
        return self.call(
            lambda *refs: None,
            (1,),
            arrays,
            [ANY] * len(arrays),
            [jax.ShapeDtypeStruct(a.shape, a.dtype) for a in arrays],
            [ANY] * len(arrays),
            aliases=[(i, i) for i in range(len(arrays))],
        )


def swiglu_grads(part_ref, second_ref, third_ref, g_ref, u_ref, out_ref):
    share = part_ref[...] + third_ref[...].astype(F32) + second_ref[...].astype(F32)
    g, u = g_ref[...], u_ref[...]
    sig = jax.nn.sigmoid(g)
    out_ref[0] = (share * u * sig * (1.0 + g * (1.0 - sig))).astype(BF)
    out_ref[1] = (share * g * sig).astype(BF)


def add_part(got_ref, part_ref, out_ref):
    out_ref[...] = (got_ref[...].astype(F32) + part_ref[...]).astype(BF)


def add_parts(second_ref, part_ref, first_ref, next_ref, third_ref, pass_ref):
    add_part(second_ref, part_ref, third_ref)
    add_part(first_ref, next_ref, pass_ref)


def partial_sums(grads_ref, w_ref, part_ref, rest_ref):
    part = dot(grads_ref[...], w_ref[...], LAST)
    part_ref[...] = part
    rest_ref[...] = part[part.shape[0] // 2 :].astype(BF)


def arrange(turn, where_ref, *refs):
    out_ref, rows = refs[4], refs[0].shape[0]
    for r, block in enumerate(refs[:4]):
        at = pl.multiple_of(place(r ^ where_ref[2], where_ref[0]) * rows, rows)
        if turn:
            out_ref[:, pl.ds(at, rows)] = block[...].T
        else:
            out_ref[pl.ds(at, rows), :] = block[...]


def first_partial_sums(where_ref, *refs):
    blocks, w_ref, part_ref, rest_ref, grads_ref = refs[:4], *refs[4:]

    @pl.when(pl.program_id(0) == 0)
    def _():
        arrange(False, where_ref, *blocks, grads_ref)

    partial_sums(grads_ref, w_ref, part_ref, rest_ref)


def hidden_values(g_ref, u_ref, out_ref):
    g = g_ref[...]
    out_ref[...] = (g * jax.nn.sigmoid(g) * u_ref[...]).astype(BF)


def joined(*pieces):
    alone = pieces[: len(pieces) % 4] if len(pieces) < 4 else pieces[:2]
    if len(pieces) == 2:
        alone = ()
    pairs = pieces[len(alone) :]
    return jnp.concatenate([*alone, *[a + b for a, b in zip(pairs[::2], pairs[1::2])]], axis=0)


def input_sums(piece_refs, held, wg_ref, wu_ref, before_ref):
    @pl.when(pl.program_id(0) == 0)
    def _():
        for which in range(2):
            held[which] = joined(*[r[which] for r in piece_refs])

    total = dot(held[0], wg_ref[...], LAST) + dot(held[1], wu_ref[...], LAST)
    return total if before_ref is None else total + before_ref[...]


def input_sums_first(count, *refs):
    refs[-2][...] = input_sums(refs[:count], refs[-1], *refs[count : count + 2], None)


def input_sums_more(count, *refs):
    refs[-2][...] = input_sums(refs[:count], refs[-1], *refs[count : count + 3])


def input_sums_last(where_ref, far_ref, end_ref, wg_ref, wu_ref, before_ref, others_ref, mine_ref, other_ref, held, total):
    rows = before_ref.shape[0]
    total[: 3 * rows, :] = others_ref[...]
    total[3 * rows :, :] = input_sums((far_ref, end_ref), held, wg_ref, wu_ref, before_ref)
    half = rows // 2
    z, core = where_ref[0], where_ref[2] % 2
    for k in range(4):
        start = place(k, z) * 2
        at = slice(k * half, (k + 1) * half)
        mine_ref[at, :] = total[pl.ds(pl.multiple_of((start + core) * half, half), half), :]
        other_ref[at, :] = total[pl.ds(pl.multiple_of((start + 1 - core) * half, half), half), :].astype(BF)


def weight_grads(inputs_ref, *refs):
    gate_ref, up_ref = refs[-2:]
    gate_ref[...] = dot(inputs_ref[...], joined(*[r[0] for r in refs[:6]]), STRAIGHT).astype(BF)
    up_ref[...] = dot(inputs_ref[...], joined(*[r[1] for r in refs[:6]]), STRAIGHT).astype(BF)


def halves(x_ref, low_ref, high_ref):
    w = low_ref.shape[2]
    low_ref[...] = x_ref[:, :, :w]
    high_ref[...] = x_ref[:, :, w:]


def down_grads(grads_ref, *refs):
    refs[-1][...] = dot(joined(*[r[...] for r in refs[:6]]), grads_ref[...], LEAD).astype(BF)


def split_again(where_ref, mine_ref, got_ref, keep_ref, y_ref, x_ref, xy_ref):
    rows = keep_ref.shape[0]
    o, half = where_ref[1], where_ref[2] // 2

    def summed(to_o, to_half):
        at = pl.ds(pl.multiple_of((2 * to_o + to_half) * rows, rows), rows)
        return mine_ref[at, :] + got_ref[at, :].astype(F32)

    keep_ref[...] = summed(o, half)
    y_ref[...] = summed(1 - o, half).astype(BF)
    x_ref[...] = summed(o, 1 - half).astype(BF)
    xy_ref[...] = summed(1 - o, 1 - half).astype(BF)


def add_last(keep_ref, y_ref, x_ref, xy_ref, out_ref):
    total = keep_ref[...] + y_ref[...].astype(F32) + x_ref[...].astype(F32) + xy_ref[...].astype(F32)
    out_ref[...] = total.astype(BF)


def shape(dims, dtype):
    return jax.ShapeDtypeStruct(dims, dtype)


def line_of_four(saved_input, saved_gate, saved_up, out_grad, w_gate, w_up, w_down):
    rows, ff = saved_gate.shape
    depth = w_gate.shape[0]
    tokens = 4 * rows
    z, o, t = lax.axis_index("inp"), lax.axis_index("out"), lax.axis_index("tok")
    where = jnp.stack([z, o, t]).astype(jnp.int32)
    chain = Chain(jnp.zeros((8, 128), F32))
    first = ff // 14 * FIRST
    cuts = [(0, first), (first, ff - first)]
    widths = [w for _, w in cuts]
    group_cuts = cuts

    def cols(height, tile, start, row=0):
        return pl.BlockSpec((height, tile), lambda j, *_: (row, start // tile + j))

    def whole(*dims):
        return pl.BlockSpec(dims, lambda *_: (0,) * len(dims))

    def tok_swaps(x):
        return x, lax.ppermute(x, "tok", CORE_SWAP), lax.ppermute(x, "tok", X_SWAP)

    def tok_last(x, sibling, other):
        (other,) = chain.relay(other)
        return x, sibling, other, lax.ppermute(other, "tok", CORE_SWAP)

    def hidden_args():
        tile = tile_of(ff, 2048)
        return (
            hidden_values,
            (ff // tile,),
            (saved_gate, saved_up),
            [cols(rows, tile, 0)] * 2,
            [shape((rows, ff), BF)],
            [cols(rows, tile, 0)],
        )

    def partial(c):
        start, w = cuts[c]
        tile = tile_of(math.gcd(start, w), 1024)
        w_spec = pl.BlockSpec((tile, depth), lambda j, *_: (start // tile + j, 0))
        outs = [shape((tokens, w), F32), shape((tokens // 2, w), BF)]
        specs = [cols(tokens, tile, 0), cols(tokens // 2, tile, 0)]
        if c:
            part, rest = chain.call(
                partial_sums, (w // tile,), (grads, w_down), [whole(tokens, depth), w_spec], outs, specs, mib=MEDIUM)
            given = grads
        else:
            part, rest, given = chain.call(
                first_partial_sums,
                (w // tile,),
                (*out_grads, w_down),
                [whole(rows, depth)] * 4 + [w_spec],
                [*outs, shape((tokens, depth), BF)],
                [*specs, whole(tokens, depth)],
                scalars=where, mib=MEDIUM)
        return given, part, send(rest, ENDS_IN)

    def pass_on(c):
        w = widths[c]
        tile = tile_of(w, 1024)
        second = chain.call(
            add_part,
            (w // tile,),
            (firsts[c], parts[c]),
            [cols(2 * rows, tile, 0), cols(2 * rows, tile, 0, 1)],
            [shape((2 * rows, w), BF)],
            [cols(2 * rows, tile, 0)],
        )[0]
        seconds[c] = send(second, MIDDLE)

    def hand_out(c):
        w = widths[c]
        third_in = [cols(rows, w, 0, 1)] * 2
        if c + 1 == len(cuts):
            third = chain.call(
                add_part, (1,), (seconds[c], parts[c]), third_in, [shape((rows, w), BF)], [whole(rows, w)]
            )[0]
        else:
            v = widths[c + 1]
            third, second = chain.call(
                add_parts,
                (1,),
                (seconds[c], parts[c], firsts[c + 1], parts[c + 1]),
                [*third_in, whole(2 * rows, v), cols(2 * rows, v, 0, 1)],
                [shape((rows, w), BF), shape((2 * rows, v), BF)],
                [whole(rows, w), whole(2 * rows, v)],
            )
            seconds[c + 1] = send(second, MIDDLE)
        thirds[c] = send(third, PAIRS)

    def grads_of(c, g):
        start, w = group_cuts[g]
        tile = tile_of(math.gcd(start, w), 1024)
        at = start - cuts[c][0]
        own = chain.call(
            swiglu_grads,
            (w // tile,),
            (parts[c], seconds[c], thirds[c], saved_gate, saved_up),
            [cols(rows, tile, at)] * 3 + [cols(rows, tile, start)] * 2,
            [shape((2, rows, w), BF)],
            [pl.BlockSpec((2, rows, tile), lambda j: (0, 0, j))],
        )[0]
        return spread(own)

    def spread(own):
        return {"own": own, "pair": send(own, PAIRS), "near": send(own, MIDDLE)}

    def spread_near(x):
        (x["near"],) = chain.relay(x["near"])
        x["near_end"] = send(x["near"], OUTWARD)

    def spread_far(x):
        (x["pair"],) = chain.relay(x["pair"])
        x["far"] = send(x["pair"], MIDDLE)

    def spread_end(x, *others):
        x["far"], *others = chain.relay(x["far"], *others)
        x["far_end"] = send(x["far"], OUTWARD)
        return others

    def pieces(x):
        return [x[k] for k in ALL]

    def input_step(g, before, names):
        start, w = group_cuts[g]
        tile = tile_of(depth, 512)
        wide = pl.BlockSpec((pl.Element(tile), pl.Element(w)), lambda j: (j * tile, start))
        count = len(names)
        height = rows * len([k for k in names if not k.endswith("_end")])
        across = cols(height, tile, 0)
        return chain.call(
            functools.partial(input_sums_first if before is None else input_sums_more, count),
            (depth // tile,),
            [*[groups[g][k] for k in names], w_gate, w_up] + ([] if before is None else [before]),
            [whole(2, rows, w)] * count + [wide, wide] + ([] if before is None else [across]),
            [shape((height, depth), F32)],
            [across],
            scratch=[pltpu.VMEM((2, height, w), BF)], mib=LARGE)[0]

    def far_more(x, cut, before):
        start, w = cut
        tile = tile_of(depth, LAST_TILE)
        wide = pl.BlockSpec((pl.Element(tile), pl.Element(w)), lambda j: (j * tile, start))
        return chain.call(
            functools.partial(input_sums_more, 2),
            (depth // tile,),
            [*x, w_gate, w_up, before],
            [whole(2, rows, w)] * 2 + [wide, wide, cols(rows, tile, 0, 3)],
            [shape((rows, depth), F32)],
            [cols(rows, tile, 0)],
            scratch=[pltpu.VMEM((2, rows, w), BF)],
            mib=LARGE,
        )[0]

    def far_last(x, cut, before, others):
        start, w = cut
        tile = tile_of(depth, LAST_TILE)
        wide = pl.BlockSpec((pl.Element(tile), pl.Element(w)), lambda j, *_: (j * tile, start))
        return chain.call(
            input_sums_last,
            (depth // tile,),
            [*x, w_gate, w_up, before, others],
            [whole(2, rows, w)] * 2 + [wide, wide, cols(rows, tile, 0), cols(3 * rows, tile, 0)],
            [shape((tokens // 2, depth), F32), shape((tokens // 2, depth), BF)],
            [cols(tokens // 2, tile, 0)] * 2,
            scalars=where,
            scratch=[pltpu.VMEM((2, rows, w), BF), pltpu.VMEM((tokens, tile), F32)],
            mib=LARGE,
        )

    def weights_step(x, cut, at, before):
        start, w = cut
        tile = tile_of(math.gcd(math.gcd(start, at), w), 1024)
        places = [at // tile if piece.shape[2] > w else 0 for piece in x]
        return chain.call(
            weight_grads,
            (w // tile,),
            (inputs, *x, *before),
            [whole(depth, tokens)]
            + [pl.BlockSpec((2, rows, tile), lambda j, p=p: (0, 0, p + j)) for p in places]
            + [ANY] * len(before),
            [shape((depth, ff), BF)] * 2,
            [cols(depth, tile, start)] * 2,
            aliases=[(7, 0), (8, 1)] if before else (),
            mib=LARGE,
        )

    def down_step():
        tile = tile_of(ff, 1024)
        return chain.call(
            down_grads,
            (ff // tile,),
            [grads, *pieces(h)],
            [whole(tokens, depth)] + [cols(rows, tile, 0)] * 6,
            [shape((ff, depth), BF)],
            [pl.BlockSpec((tile, depth), lambda j, *_: (j, 0))], mib=MEDIUM)[0]

    n = len(cuts)
    parts, firsts, seconds, thirds = ([None] * n for _ in range(4))
    out_grads = tok_swaps(out_grad)
    h = spread(Chain(jnp.zeros((8, 128), F32)).call(*hidden_args(), mib=WHOLE)[0])
    out_grads = tok_last(*out_grads)
    grads, parts[0], firsts[0] = partial(0)
    _, parts[1], firsts[1] = partial(1)
    spread_near(h)
    spread_far(h)
    pass_on(0)
    (h["near_end"],) = spread_end(h, h["near_end"])
    hand_out(0)
    (h["far_end"],) = chain.relay(h["far_end"])
    groups = [grads_of(0, 0)]
    down = down_step()
    hand_out(1)
    spread_far(groups[0])
    (thirds[1],) = chain.relay(thirds[1])
    spread_near(groups[0])
    groups.append(grads_of(1, 1))
    spread_end(groups[0])
    (groups[0]["near_end"],) = chain.relay(groups[0]["near_end"])
    (inputs_b,) = chain.relay(saved_input.astype(BF))
    in_raw = tok_last(*tok_swaps(inputs_b))
    inputs = chain.call(
        functools.partial(arrange, True),
        (1,),
        in_raw,
        [whole(rows, depth)] * 4,
        [shape((depth, tokens), BF)],
        [whole(depth, tokens)],
        scalars=where,
    )[0]
    spread_near(groups[1])
    spread_far(groups[1])
    (groups[0]["far_end"],) = chain.relay(groups[0]["far_end"])
    total = input_step(0, None, ALL)
    weights = weights_step(pieces(groups[0]), cuts[0], 0, ())
    second = ff - first
    part = second // 2
    low_cut, high_cut = (first, part), (first + part, part)
    low, high = chain.call(
        halves,
        (1,),
        (groups[1]["far"],),
        [whole(2, rows, second)],
        [shape((2, rows, part), BF)] * 2,
        [whole(2, rows, part)] * 2,
    )
    low, high = (low, send(low, OUTWARD)), (high, send(high, OUTWARD))
    early = [groups[1][k] for k in ALL[:4]]
    others = input_step(1, total, ALL[:4])
    total = far_more(low, low_cut, total)
    weights = weights_step([*early, *low], low_cut, 0, weights)
    mine, other = far_last(high, high_cut, total, others)
    got = lax.ppermute(other, "tok", CORE_SWAP)
    keep, *others = chain.call(
        split_again,
        (1,),
        (mine, got),
        [whole(tokens // 2, depth)] * 2,
        [shape((rows // 2, depth), F32), *[shape((rows // 2, depth), BF)] * 3],
        [whole(rows // 2, depth)] * 4,
        scalars=where,
    )
    got = (
        lax.ppermute(others[2], ("out", "tok"), XY_SWAP),
        lax.ppermute(others[0], "out", Y_SWAP),
        lax.ppermute(others[1], "tok", X_SWAP),
    )
    weights = weights_step([*early, *high], high_cut, part, weights)
    result = chain.call(
        add_last,
        (1,),
        (keep, got[1], got[2], got[0]),
        [whole(rows // 2, depth)] * 4,
        [shape((rows // 2, depth), BF)],
        [whole(rows // 2, depth)],
    )[0]
    return result, weights[0], weights[1], down


def any_line(saved_input, saved_gate, saved_up, out_grad, w_gate, w_up, w_down):
    inputs = lax.all_gather(saved_input.astype(BF), "tok", axis=0, tiled=True)
    grads = lax.all_gather(out_grad, "tok", axis=0, tiled=True)
    part = dot(grads, w_down, LAST)
    share = lax.psum_scatter(part, "inp", scatter_dimension=0, tiled=True)
    sig = jax.nn.sigmoid(saved_gate)
    gate = share * saved_up * sig * (1.0 + saved_gate * (1.0 - sig))
    up = share * saved_gate * sig
    hidden = saved_gate * sig * saved_up
    gate, up, hidden = (
        lax.all_gather(v.astype(BF), "inp", axis=0, tiled=True) for v in (gate, up, hidden)
    )
    total = dot(gate, w_gate, LAST) + dot(up, w_up, LAST)
    total = lax.psum_scatter(total, ("out", "tok"), scatter_dimension=0, tiled=True)
    return (
        total.astype(BF),
        dot(inputs, gate, LEAD).astype(BF),
        dot(inputs, up, LEAD).astype(BF),
        dot(hidden, grads, LEAD).astype(BF),
    )


def solution(mesh):
    sizes = dict(mesh.shape)
    placed = (
        P("tok", "inp"),
        P("inp", ("out", "tok")),
        P("inp", ("out", "tok")),
        P("tok", "inp"),
        P("inp", ("out", "tok")),
        P("inp", ("out", "tok")),
        P(("out", "tok"), "inp"),
    )

    def local(*args):
        rows, ff = args[1].shape
        fits = (sizes["inp"], sizes["out"], sizes["tok"]) == (4, 2, 4)
        if fits and rows % 32 == 0 and ff % 3584 == 0:
            return line_of_four(*args)
        return any_line(*args)

    return jax.shard_map(
        local,
        mesh=mesh,
        in_specs=placed,
        out_specs=(
            P(("out", "tok"), "inp"),
            P("inp", ("out", "tok")),
            P("inp", ("out", "tok")),
            P(("out", "tok"), "inp"),
        ),
        check_vma=False,
    )
```

```python
import functools
import math

import jax
import jax.numpy as jnp
from jax import lax
from jax.experimental import pallas as pl
from jax.experimental.pallas import tpu as pltpu
from jax.sharding import PartitionSpec as P

BF, F32 = jnp.bfloat16, jnp.float32
LAST = (((1,), (1,)), ((), ()))
LEAD = (((0,), (0,)), ((), ()))
STRAIGHT = (((1,), (0,)), ((), ()))
ANY = pl.BlockSpec(memory_space=pl.ANY)
MIB = 1024 * 1024
SMALL, MEDIUM, LARGE, WHOLE = 8, 16, 28, 62

ENDS_IN = [(0, 1), (3, 2)]
MIDDLE = [(1, 2), (2, 1)]
PAIRS = [(0, 1), (1, 0), (2, 3), (3, 2)]
OUTWARD = [(1, 0), (2, 3)]
X_SWAP = [(0, 2), (2, 0), (1, 3), (3, 1)]
CORE_SWAP = [(0, 1), (1, 0), (2, 3), (3, 2)]
Y_SWAP = [(0, 1), (1, 0)]
XY_SWAP = [(4 * o + t, 4 * (1 - o) + (t ^ 2)) for o in range(2) for t in range(4)]


def send(x, perm):
    return lax.ppermute(x, "inp", perm)


LAST_TILE = 1024
FIRST = 7
ALL = ("own", "pair", "near", "near_end", "far", "far_end")


def tile_of(size, most):
    return max(t for t in range(128, most + 1, 128) if size % t == 0)


def place(k, z):
    return jnp.where(k // 2 == z // 2, k ^ z, jnp.where(z < 2, k, 3 - k))


def dot(a, b, dims):
    return lax.dot_general(a, b, dims, preferred_element_type=F32)


class Chain:
    def __init__(self, token):
        self.token = token

    def call(self, body, grid, ins, in_specs, outs, out_specs, aliases=(), scalars=None, scratch=(), mib=SMALL):
        lead = 0 if scalars is None else 1

        def kernel(*refs):
            body(*refs[:lead], *refs[lead + 1 : lead + 1 + len(ins)], *refs[lead + 2 + len(ins) :])

        pairs = {lead: 0, **{lead + 1 + i: 1 + o for i, o in aliases}}
        given = pl.pallas_call(
            kernel,
            grid_spec=pltpu.PrefetchScalarGridSpec(
                num_scalar_prefetch=lead,
                grid=grid,
                in_specs=[ANY, *in_specs],
                out_specs=[ANY, *out_specs],
                scratch_shapes=list(scratch),
            ),
            out_shape=[jax.ShapeDtypeStruct(self.token.shape, self.token.dtype), *outs],
            input_output_aliases=pairs,
            compiler_params=pltpu.CompilerParams(vmem_limit_bytes=mib * MIB),
        )(*(() if scalars is None else (scalars,)), self.token, *ins)
        self.token = given[0]
        return given[1:]

    def relay(self, *arrays):
        return self.call(
            lambda *refs: None,
            (1,),
            arrays,
            [ANY] * len(arrays),
            [jax.ShapeDtypeStruct(a.shape, a.dtype) for a in arrays],
            [ANY] * len(arrays),
            aliases=[(i, i) for i in range(len(arrays))],
        )


def swiglu_grads(part_ref, second_ref, third_ref, g_ref, u_ref, out_ref):
    share = part_ref[...] + third_ref[...].astype(F32) + second_ref[...].astype(F32)
    g, u = g_ref[...], u_ref[...]
    sig = jax.nn.sigmoid(g)
    out_ref[0] = (share * u * sig * (1.0 + g * (1.0 - sig))).astype(BF)
    out_ref[1] = (share * g * sig).astype(BF)


def add_part(got_ref, part_ref, out_ref):
    out_ref[...] = (got_ref[...].astype(F32) + part_ref[...]).astype(BF)


def add_parts(second_ref, part_ref, first_ref, next_ref, third_ref, pass_ref):
    add_part(second_ref, part_ref, third_ref)
    add_part(first_ref, next_ref, pass_ref)


def partial_sums(grads_ref, w_ref, part_ref, rest_ref):
    part = dot(grads_ref[...], w_ref[...], LAST)
    part_ref[...] = part
    rest_ref[...] = part[part.shape[0] // 2 :].astype(BF)


def arrange(turn, where_ref, *refs):
    out_ref, rows = refs[4], refs[0].shape[0]
    for r, block in enumerate(refs[:4]):
        at = pl.multiple_of(place(r ^ where_ref[2], where_ref[0]) * rows, rows)
        if turn:
            out_ref[:, pl.ds(at, rows)] = block[...].T
        else:
            out_ref[pl.ds(at, rows), :] = block[...]


def first_partial_sums(where_ref, *refs):
    blocks, w_ref, part_ref, rest_ref, grads_ref = refs[:4], *refs[4:]

    @pl.when(pl.program_id(0) == 0)
    def _():
        arrange(False, where_ref, *blocks, grads_ref)

    partial_sums(grads_ref, w_ref, part_ref, rest_ref)


def hidden_values(g_ref, u_ref, out_ref):
    g = g_ref[...]
    out_ref[...] = (g * jax.nn.sigmoid(g) * u_ref[...]).astype(BF)


def joined(*pieces):
    alone = pieces[: len(pieces) % 4] if len(pieces) < 4 else pieces[:2]
    if len(pieces) == 2:
        alone = ()
    pairs = pieces[len(alone) :]
    return jnp.concatenate([*alone, *[a + b for a, b in zip(pairs[::2], pairs[1::2])]], axis=0)


def input_sums(piece_refs, held, wg_ref, wu_ref, before_ref):
    @pl.when(pl.program_id(0) == 0)
    def _():
        for which in range(2):
            held[which] = joined(*[r[which] for r in piece_refs])

    total = dot(held[0], wg_ref[...], LAST) + dot(held[1], wu_ref[...], LAST)
    return total if before_ref is None else total + before_ref[...]


def input_sums_first(count, *refs):
    refs[-2][...] = input_sums(refs[:count], refs[-1], *refs[count : count + 2], None)


def input_sums_more(count, *refs):
    refs[-2][...] = input_sums(refs[:count], refs[-1], *refs[count : count + 3])


def input_sums_last(where_ref, far_ref, end_ref, wg_ref, wu_ref, before_ref, others_ref, mine_ref, other_ref, held, total):
    rows = before_ref.shape[0]
    total[: 3 * rows, :] = others_ref[...]
    total[3 * rows :, :] = input_sums((far_ref, end_ref), held, wg_ref, wu_ref, before_ref)
    half = rows // 2
    z, core = where_ref[0], where_ref[2] % 2
    for k in range(4):
        start = place(k, z) * 2
        at = slice(k * half, (k + 1) * half)
        mine_ref[at, :] = total[pl.ds(pl.multiple_of((start + core) * half, half), half), :]
        other_ref[at, :] = total[pl.ds(pl.multiple_of((start + 1 - core) * half, half), half), :].astype(BF)


def weight_grads(inputs_ref, *refs):
    gate_ref, up_ref = refs[-2:]
    gate_ref[...] = dot(inputs_ref[...], joined(*[r[0] for r in refs[:6]]), STRAIGHT).astype(BF)
    up_ref[...] = dot(inputs_ref[...], joined(*[r[1] for r in refs[:6]]), STRAIGHT).astype(BF)


def halves(x_ref, low_ref, high_ref):
    w = low_ref.shape[2]
    low_ref[...] = x_ref[:, :, :w]
    high_ref[...] = x_ref[:, :, w:]


def down_grads(grads_ref, *refs):
    refs[-1][...] = dot(joined(*[r[...] for r in refs[:6]]), grads_ref[...], LEAD).astype(BF)


def split_again(where_ref, mine_ref, got_ref, keep_ref, y_ref, x_ref, xy_ref):
    rows = keep_ref.shape[0]
    o, half = where_ref[1], where_ref[2] // 2

    def summed(to_o, to_half):
        at = pl.ds(pl.multiple_of((2 * to_o + to_half) * rows, rows), rows)
        return mine_ref[at, :] + got_ref[at, :].astype(F32)

    keep_ref[...] = summed(o, half)
    y_ref[...] = summed(1 - o, half).astype(BF)
    x_ref[...] = summed(o, 1 - half).astype(BF)
    xy_ref[...] = summed(1 - o, 1 - half).astype(BF)


def add_last(keep_ref, y_ref, x_ref, xy_ref, out_ref):
    total = keep_ref[...] + y_ref[...].astype(F32) + x_ref[...].astype(F32) + xy_ref[...].astype(F32)
    out_ref[...] = total.astype(BF)


def shape(dims, dtype):
    return jax.ShapeDtypeStruct(dims, dtype)


def line_of_four(saved_input, saved_gate, saved_up, out_grad, w_gate, w_up, w_down):
    rows, ff = saved_gate.shape
    depth = w_gate.shape[0]
    tokens = 4 * rows
    z, o, t = lax.axis_index("inp"), lax.axis_index("out"), lax.axis_index("tok")
    where = jnp.stack([z, o, t]).astype(jnp.int32)
    chain = Chain(jnp.zeros((8, 128), F32))
    first = ff // 14 * FIRST
    cuts = [(0, first), (first, ff - first)]
    widths = [w for _, w in cuts]
    group_cuts = cuts

    def cols(height, tile, start, row=0):
        return pl.BlockSpec((height, tile), lambda j, *_: (row, start // tile + j))

    def whole(*dims):
        return pl.BlockSpec(dims, lambda *_: (0,) * len(dims))

    def tok_swaps(x):
        return x, lax.ppermute(x, "tok", CORE_SWAP), lax.ppermute(x, "tok", X_SWAP)

    def tok_last(x, sibling, other):
        (other,) = chain.relay(other)
        return x, sibling, other, lax.ppermute(other, "tok", CORE_SWAP)

    def hidden_args():
        tile = tile_of(ff, 2048)
        return (
            hidden_values,
            (ff // tile,),
            (saved_gate, saved_up),
            [cols(rows, tile, 0)] * 2,
            [shape((rows, ff), BF)],
            [cols(rows, tile, 0)],
        )

    def partial(c):
        start, w = cuts[c]
        tile = tile_of(math.gcd(start, w), 1024)
        w_spec = pl.BlockSpec((tile, depth), lambda j, *_: (start // tile + j, 0))
        outs = [shape((tokens, w), F32), shape((tokens // 2, w), BF)]
        specs = [cols(tokens, tile, 0), cols(tokens // 2, tile, 0)]
        if c:
            part, rest = chain.call(
                partial_sums, (w // tile,), (grads, w_down), [whole(tokens, depth), w_spec], outs, specs, mib=MEDIUM)
            given = grads
        else:
            part, rest, given = chain.call(
                first_partial_sums,
                (w // tile,),
                (*out_grads, w_down),
                [whole(rows, depth)] * 4 + [w_spec],
                [*outs, shape((tokens, depth), BF)],
                [*specs, whole(tokens, depth)],
                scalars=where, mib=MEDIUM)
        return given, part, send(rest, ENDS_IN)

    def pass_on(c):
        w = widths[c]
        tile = tile_of(w, 1024)
        second = chain.call(
            add_part,
            (w // tile,),
            (firsts[c], parts[c]),
            [cols(2 * rows, tile, 0), cols(2 * rows, tile, 0, 1)],
            [shape((2 * rows, w), BF)],
            [cols(2 * rows, tile, 0)],
        )[0]
        seconds[c] = send(second, MIDDLE)

    def hand_out(c):
        w = widths[c]
        third_in = [cols(rows, w, 0, 1)] * 2
        if c + 1 == len(cuts):
            third = chain.call(
                add_part, (1,), (seconds[c], parts[c]), third_in, [shape((rows, w), BF)], [whole(rows, w)]
            )[0]
        else:
            v = widths[c + 1]
            third, second = chain.call(
                add_parts,
                (1,),
                (seconds[c], parts[c], firsts[c + 1], parts[c + 1]),
                [*third_in, whole(2 * rows, v), cols(2 * rows, v, 0, 1)],
                [shape((rows, w), BF), shape((2 * rows, v), BF)],
                [whole(rows, w), whole(2 * rows, v)],
            )
            seconds[c + 1] = send(second, MIDDLE)
        thirds[c] = send(third, PAIRS)

    def grads_of(c, g):
        start, w = group_cuts[g]
        tile = tile_of(math.gcd(start, w), 1024)
        at = start - cuts[c][0]
        own = chain.call(
            swiglu_grads,
            (w // tile,),
            (parts[c], seconds[c], thirds[c], saved_gate, saved_up),
            [cols(rows, tile, at)] * 3 + [cols(rows, tile, start)] * 2,
            [shape((2, rows, w), BF)],
            [pl.BlockSpec((2, rows, tile), lambda j: (0, 0, j))],
        )[0]
        return spread(own)

    def spread(own):
        return {"own": own, "pair": send(own, PAIRS), "near": send(own, MIDDLE)}

    def spread_near(x):
        (x["near"],) = chain.relay(x["near"])
        x["near_end"] = send(x["near"], OUTWARD)

    def spread_far(x):
        (x["pair"],) = chain.relay(x["pair"])
        x["far"] = send(x["pair"], MIDDLE)

    def spread_end(x, *others):
        x["far"], *others = chain.relay(x["far"], *others)
        x["far_end"] = send(x["far"], OUTWARD)
        return others

    def pieces(x):
        return [x[k] for k in ALL]

    def input_step(g, before, names):
        start, w = group_cuts[g]
        tile = tile_of(depth, 1024)
        wide = pl.BlockSpec((pl.Element(tile), pl.Element(w)), lambda j: (j * tile, start))
        count = len(names)
        height = rows * len([k for k in names if not k.endswith("_end")])
        across = cols(height, tile, 0)
        return chain.call(
            functools.partial(input_sums_first if before is None else input_sums_more, count),
            (depth // tile,),
            [*[groups[g][k] for k in names], w_gate, w_up] + ([] if before is None else [before]),
            [whole(2, rows, w)] * count + [wide, wide] + ([] if before is None else [across]),
            [shape((height, depth), F32)],
            [across],
            scratch=[pltpu.VMEM((2, height, w), BF)], mib=LARGE)[0]

    def far_more(x, cut, before):
        start, w = cut
        tile = tile_of(depth, LAST_TILE)
        wide = pl.BlockSpec((pl.Element(tile), pl.Element(w)), lambda j: (j * tile, start))
        return chain.call(
            functools.partial(input_sums_more, 2),
            (depth // tile,),
            [*x, w_gate, w_up, before],
            [whole(2, rows, w)] * 2 + [wide, wide, cols(rows, tile, 0, 3)],
            [shape((rows, depth), F32)],
            [cols(rows, tile, 0)],
            scratch=[pltpu.VMEM((2, rows, w), BF)],
            mib=LARGE,
        )[0]

    def far_last(x, cut, before, others):
        start, w = cut
        tile = tile_of(depth, LAST_TILE)
        wide = pl.BlockSpec((pl.Element(tile), pl.Element(w)), lambda j, *_: (j * tile, start))
        return chain.call(
            input_sums_last,
            (depth // tile,),
            [*x, w_gate, w_up, before, others],
            [whole(2, rows, w)] * 2 + [wide, wide, cols(rows, tile, 0), cols(3 * rows, tile, 0)],
            [shape((tokens // 2, depth), F32), shape((tokens // 2, depth), BF)],
            [cols(tokens // 2, tile, 0)] * 2,
            scalars=where,
            scratch=[pltpu.VMEM((2, rows, w), BF), pltpu.VMEM((tokens, tile), F32)],
            mib=LARGE,
        )

    def weights_step(x, cut, at, before):
        start, w = cut
        tile = tile_of(math.gcd(math.gcd(start, at), w), 1024)
        places = [at // tile if piece.shape[2] > w else 0 for piece in x]
        return chain.call(
            weight_grads,
            (w // tile,),
            (inputs, *x, *before),
            [whole(depth, tokens)]
            + [pl.BlockSpec((2, rows, tile), lambda j, p=p: (0, 0, p + j)) for p in places]
            + [ANY] * len(before),
            [shape((depth, ff), BF)] * 2,
            [cols(depth, tile, start)] * 2,
            aliases=[(7, 0), (8, 1)] if before else (),
            mib=LARGE,
        )

    def down_step():
        tile = tile_of(ff, 1024)
        return chain.call(
            down_grads,
            (ff // tile,),
            [grads, *pieces(h)],
            [whole(tokens, depth)] + [cols(rows, tile, 0)] * 6,
            [shape((ff, depth), BF)],
            [pl.BlockSpec((tile, depth), lambda j, *_: (j, 0))], mib=MEDIUM)[0]

    n = len(cuts)
    parts, firsts, seconds, thirds = ([None] * n for _ in range(4))
    out_grads = tok_swaps(out_grad)
    h = spread(Chain(jnp.zeros((8, 128), F32)).call(*hidden_args(), mib=WHOLE)[0])
    out_grads = tok_last(*out_grads)
    grads, parts[0], firsts[0] = partial(0)
    spread_near(h)
    spread_far(h)
    _, parts[1], firsts[1] = partial(1)
    pass_on(0)
    (h["near_end"],) = spread_end(h, h["near_end"])
    hand_out(0)
    (h["far_end"],) = chain.relay(h["far_end"])
    groups = [grads_of(0, 0)]
    down = down_step()
    hand_out(1)
    spread_far(groups[0])
    (thirds[1],) = chain.relay(thirds[1])
    spread_near(groups[0])
    groups.append(grads_of(1, 1))
    spread_end(groups[0])
    (groups[0]["near_end"],) = chain.relay(groups[0]["near_end"])
    (inputs_b,) = chain.relay(saved_input.astype(BF))
    in_raw = tok_last(*tok_swaps(inputs_b))
    inputs = chain.call(
        functools.partial(arrange, True),
        (1,),
        in_raw,
        [whole(rows, depth)] * 4,
        [shape((depth, tokens), BF)],
        [whole(depth, tokens)],
        scalars=where,
    )[0]
    spread_near(groups[1])
    spread_far(groups[1])
    (groups[0]["far_end"],) = chain.relay(groups[0]["far_end"])
    total = input_step(0, None, ALL)
    weights = weights_step(pieces(groups[0]), cuts[0], 0, ())
    second = ff - first
    part = second // 2
    low_cut, high_cut = (first, part), (first + part, part)
    low, high = chain.call(
        halves,
        (1,),
        (groups[1]["far"],),
        [whole(2, rows, second)],
        [shape((2, rows, part), BF)] * 2,
        [whole(2, rows, part)] * 2,
    )
    low, high = (low, send(low, OUTWARD)), (high, send(high, OUTWARD))
    early = [groups[1][k] for k in ALL[:4]]
    others = input_step(1, total, ALL[:4])
    total = far_more(low, low_cut, total)
    weights = weights_step([*early, *low], low_cut, 0, weights)
    mine, other = far_last(high, high_cut, total, others)
    got = lax.ppermute(other, "tok", CORE_SWAP)
    keep, *others = chain.call(
        split_again,
        (1,),
        (mine, got),
        [whole(tokens // 2, depth)] * 2,
        [shape((rows // 2, depth), F32), *[shape((rows // 2, depth), BF)] * 3],
        [whole(rows // 2, depth)] * 4,
        scalars=where,
    )
    got = (
        lax.ppermute(others[2], ("out", "tok"), XY_SWAP),
        lax.ppermute(others[0], "out", Y_SWAP),
        lax.ppermute(others[1], "tok", X_SWAP),
    )
    weights = weights_step([*early, *high], high_cut, part, weights)
    result = chain.call(
        add_last,
        (1,),
        (keep, got[1], got[2], got[0]),
        [whole(rows // 2, depth)] * 4,
        [shape((rows // 2, depth), BF)],
        [whole(rows // 2, depth)],
    )[0]
    return result, weights[0], weights[1], down


def any_line(saved_input, saved_gate, saved_up, out_grad, w_gate, w_up, w_down):
    inputs = lax.all_gather(saved_input.astype(BF), "tok", axis=0, tiled=True)
    grads = lax.all_gather(out_grad, "tok", axis=0, tiled=True)
    part = dot(grads, w_down, LAST)
    share = lax.psum_scatter(part, "inp", scatter_dimension=0, tiled=True)
    sig = jax.nn.sigmoid(saved_gate)
    gate = share * saved_up * sig * (1.0 + saved_gate * (1.0 - sig))
    up = share * saved_gate * sig
    hidden = saved_gate * sig * saved_up
    gate, up, hidden = (
        lax.all_gather(v.astype(BF), "inp", axis=0, tiled=True) for v in (gate, up, hidden)
    )
    total = dot(gate, w_gate, LAST) + dot(up, w_up, LAST)
    total = lax.psum_scatter(total, ("out", "tok"), scatter_dimension=0, tiled=True)
    return (
        total.astype(BF),
        dot(inputs, gate, LEAD).astype(BF),
        dot(inputs, up, LEAD).astype(BF),
        dot(hidden, grads, LEAD).astype(BF),
    )


def solution(mesh):
    sizes = dict(mesh.shape)
    placed = (
        P("tok", "inp"),
        P("inp", ("out", "tok")),
        P("inp", ("out", "tok")),
        P("tok", "inp"),
        P("inp", ("out", "tok")),
        P("inp", ("out", "tok")),
        P(("out", "tok"), "inp"),
    )

    def local(*args):
        rows, ff = args[1].shape
        fits = (sizes["inp"], sizes["out"], sizes["tok"]) == (4, 2, 4)
        if fits and rows % 32 == 0 and ff % 3584 == 0:
            return line_of_four(*args)
        return any_line(*args)

    return jax.shard_map(
        local,
        mesh=mesh,
        in_specs=placed,
        out_specs=(
            P(("out", "tok"), "inp"),
            P("inp", ("out", "tok")),
            P("inp", ("out", "tok")),
            P(("out", "tok"), "inp"),
        ),
        check_vma=False,
    )
```

```python
import functools
import math

import jax
import jax.numpy as jnp
from jax import lax
from jax.experimental import pallas as pl
from jax.experimental.pallas import tpu as pltpu
from jax.sharding import PartitionSpec as P

BF, F32 = jnp.bfloat16, jnp.float32
LAST = (((1,), (1,)), ((), ()))
LEAD = (((0,), (0,)), ((), ()))
STRAIGHT = (((1,), (0,)), ((), ()))
ANY = pl.BlockSpec(memory_space=pl.ANY)
MIB = 1024 * 1024
SMALL, MEDIUM, LARGE, WHOLE = 8, 16, 28, 62

ENDS_IN = [(0, 1), (3, 2)]
MIDDLE = [(1, 2), (2, 1)]
PAIRS = [(0, 1), (1, 0), (2, 3), (3, 2)]
OUTWARD = [(1, 0), (2, 3)]
X_SWAP = [(0, 2), (2, 0), (1, 3), (3, 1)]
CORE_SWAP = [(0, 1), (1, 0), (2, 3), (3, 2)]
Y_SWAP = [(0, 1), (1, 0)]
XY_SWAP = [(4 * o + t, 4 * (1 - o) + (t ^ 2)) for o in range(2) for t in range(4)]


def send(x, perm):
    return lax.ppermute(x, "inp", perm)


LAST_TILE = 1024
FIRST = 7
ALL = ("own", "pair", "near", "near_end", "far", "far_end")


def tile_of(size, most):
    return max(t for t in range(128, most + 1, 128) if size % t == 0)


def place(k, z):
    return jnp.where(k // 2 == z // 2, k ^ z, jnp.where(z < 2, k, 3 - k))


def dot(a, b, dims):
    return lax.dot_general(a, b, dims, preferred_element_type=F32)


class Chain:
    def __init__(self, token):
        self.token = token

    def call(self, body, grid, ins, in_specs, outs, out_specs, aliases=(), scalars=None, scratch=(), mib=SMALL):
        lead = 0 if scalars is None else 1

        def kernel(*refs):
            body(*refs[:lead], *refs[lead + 1 : lead + 1 + len(ins)], *refs[lead + 2 + len(ins) :])

        pairs = {lead: 0, **{lead + 1 + i: 1 + o for i, o in aliases}}
        given = pl.pallas_call(
            kernel,
            grid_spec=pltpu.PrefetchScalarGridSpec(
                num_scalar_prefetch=lead,
                grid=grid,
                in_specs=[ANY, *in_specs],
                out_specs=[ANY, *out_specs],
                scratch_shapes=list(scratch),
            ),
            out_shape=[jax.ShapeDtypeStruct(self.token.shape, self.token.dtype), *outs],
            input_output_aliases=pairs,
            compiler_params=pltpu.CompilerParams(vmem_limit_bytes=mib * MIB),
        )(*(() if scalars is None else (scalars,)), self.token, *ins)
        self.token = given[0]
        return given[1:]

    def relay(self, *arrays):
        return self.call(
            lambda *refs: None,
            (1,),
            arrays,
            [ANY] * len(arrays),
            [jax.ShapeDtypeStruct(a.shape, a.dtype) for a in arrays],
            [ANY] * len(arrays),
            aliases=[(i, i) for i in range(len(arrays))],
        )


def swiglu_grads(part_ref, second_ref, third_ref, g_ref, u_ref, out_ref):
    share = part_ref[...] + third_ref[...].astype(F32) + second_ref[...].astype(F32)
    g, u = g_ref[...], u_ref[...]
    sig = jax.nn.sigmoid(g)
    out_ref[0] = (share * u * sig * (1.0 + g * (1.0 - sig))).astype(BF)
    out_ref[1] = (share * g * sig).astype(BF)


def add_part(got_ref, part_ref, out_ref):
    out_ref[...] = (got_ref[...].astype(F32) + part_ref[...]).astype(BF)


def add_parts(second_ref, part_ref, first_ref, next_ref, third_ref, pass_ref):
    add_part(second_ref, part_ref, third_ref)
    add_part(first_ref, next_ref, pass_ref)


def partial_sums(grads_ref, w_ref, part_ref, rest_ref):
    part = dot(grads_ref[...], w_ref[...], LAST)
    part_ref[...] = part
    rest_ref[...] = part[part.shape[0] // 2 :].astype(BF)


def arrange(turn, where_ref, *refs):
    out_ref, rows = refs[4], refs[0].shape[0]
    for r, block in enumerate(refs[:4]):
        at = pl.multiple_of(place(r ^ where_ref[2], where_ref[0]) * rows, rows)
        if turn:
            out_ref[:, pl.ds(at, rows)] = block[...].T
        else:
            out_ref[pl.ds(at, rows), :] = block[...]


def first_partial_sums(where_ref, *refs):
    blocks, w_ref, part_ref, rest_ref, grads_ref = refs[:4], *refs[4:]

    @pl.when(pl.program_id(0) == 0)
    def _():
        arrange(False, where_ref, *blocks, grads_ref)

    partial_sums(grads_ref, w_ref, part_ref, rest_ref)


def hidden_values(g_ref, u_ref, out_ref):
    g = g_ref[...]
    out_ref[...] = (g * jax.nn.sigmoid(g) * u_ref[...]).astype(BF)


def joined(*pieces):
    alone = pieces[: len(pieces) % 4] if len(pieces) < 4 else pieces[:2]
    if len(pieces) == 2:
        alone = ()
    pairs = pieces[len(alone) :]
    return jnp.concatenate([*alone, *[a + b for a, b in zip(pairs[::2], pairs[1::2])]], axis=0)


def input_sums(piece_refs, held, wg_ref, wu_ref, before_ref):
    @pl.when(pl.program_id(0) == 0)
    def _():
        for which in range(2):
            held[which] = joined(*[r[which] for r in piece_refs])

    total = dot(held[0], wg_ref[...], LAST) + dot(held[1], wu_ref[...], LAST)
    return total if before_ref is None else total + before_ref[...]


def input_sums_first(count, *refs):
    refs[-2][...] = input_sums(refs[:count], refs[-1], *refs[count : count + 2], None)


def input_sums_more(count, *refs):
    refs[-2][...] = input_sums(refs[:count], refs[-1], *refs[count : count + 3])


def input_sums_last(where_ref, far_ref, end_ref, wg_ref, wu_ref, before_ref, others_ref, mine_ref, other_ref, held, total):
    rows = before_ref.shape[0]
    total[: 3 * rows, :] = others_ref[...]
    total[3 * rows :, :] = input_sums((far_ref, end_ref), held, wg_ref, wu_ref, before_ref)
    half = rows // 2
    z, core = where_ref[0], where_ref[2] % 2
    for k in range(4):
        start = place(k, z) * 2
        at = slice(k * half, (k + 1) * half)
        mine_ref[at, :] = total[pl.ds(pl.multiple_of((start + core) * half, half), half), :]
        other_ref[at, :] = total[pl.ds(pl.multiple_of((start + 1 - core) * half, half), half), :].astype(BF)


def weight_grads(inputs_ref, *refs):
    gate_ref, up_ref = refs[-2:]
    gate_ref[...] = dot(inputs_ref[...], joined(*[r[0] for r in refs[:6]]), STRAIGHT).astype(BF)
    up_ref[...] = dot(inputs_ref[...], joined(*[r[1] for r in refs[:6]]), STRAIGHT).astype(BF)


def halves(x_ref, low_ref, high_ref):
    w = low_ref.shape[2]
    low_ref[...] = x_ref[:, :, :w]
    high_ref[...] = x_ref[:, :, w:]


def down_grads(grads_ref, *refs):
    refs[-1][...] = dot(joined(*[r[...] for r in refs[:6]]), grads_ref[...], LEAD).astype(BF)


def split_again(where_ref, mine_ref, got_ref, keep_ref, y_ref, x_ref, xy_ref):
    rows = keep_ref.shape[0]
    o, half = where_ref[1], where_ref[2] // 2

    def summed(to_o, to_half):
        at = pl.ds(pl.multiple_of((2 * to_o + to_half) * rows, rows), rows)
        return mine_ref[at, :] + got_ref[at, :].astype(F32)

    keep_ref[...] = summed(o, half)
    y_ref[...] = summed(1 - o, half).astype(BF)
    x_ref[...] = summed(o, 1 - half).astype(BF)
    xy_ref[...] = summed(1 - o, 1 - half).astype(BF)


def add_last(keep_ref, y_ref, x_ref, xy_ref, out_ref):
    total = keep_ref[...] + y_ref[...].astype(F32) + x_ref[...].astype(F32) + xy_ref[...].astype(F32)
    out_ref[...] = total.astype(BF)


def shape(dims, dtype):
    return jax.ShapeDtypeStruct(dims, dtype)


def line_of_four(saved_input, saved_gate, saved_up, out_grad, w_gate, w_up, w_down):
    rows, ff = saved_gate.shape
    depth = w_gate.shape[0]
    tokens = 4 * rows
    z, o, t = lax.axis_index("inp"), lax.axis_index("out"), lax.axis_index("tok")
    where = jnp.stack([z, o, t]).astype(jnp.int32)
    chain = Chain(jnp.zeros((8, 128), F32))
    first = ff // 14 * FIRST
    cuts = [(0, first), (first, ff - first)]
    widths = [w for _, w in cuts]
    group_cuts = cuts

    def cols(height, tile, start, row=0):
        return pl.BlockSpec((height, tile), lambda j, *_: (row, start // tile + j))

    def whole(*dims):
        return pl.BlockSpec(dims, lambda *_: (0,) * len(dims))

    def tok_swaps(x):
        return x, lax.ppermute(x, "tok", CORE_SWAP), lax.ppermute(x, "tok", X_SWAP)

    def tok_last(x, sibling, other):
        (other,) = chain.relay(other)
        return x, sibling, other, lax.ppermute(other, "tok", CORE_SWAP)

    def hidden_args():
        tile = tile_of(ff, 2048)
        return (
            hidden_values,
            (ff // tile,),
            (saved_gate, saved_up),
            [cols(rows, tile, 0)] * 2,
            [shape((rows, ff), BF)],
            [cols(rows, tile, 0)],
        )

    def partial(c):
        start, w = cuts[c]
        tile = tile_of(math.gcd(start, w), 1024)
        w_spec = pl.BlockSpec((tile, depth), lambda j, *_: (start // tile + j, 0))
        outs = [shape((tokens, w), F32), shape((tokens // 2, w), BF)]
        specs = [cols(tokens, tile, 0), cols(tokens // 2, tile, 0)]
        if c:
            part, rest = chain.call(
                partial_sums, (w // tile,), (grads, w_down), [whole(tokens, depth), w_spec], outs, specs, mib=MEDIUM)
            given = grads
        else:
            part, rest, given = chain.call(
                first_partial_sums,
                (w // tile,),
                (*out_grads, w_down),
                [whole(rows, depth)] * 4 + [w_spec],
                [*outs, shape((tokens, depth), BF)],
                [*specs, whole(tokens, depth)],
                scalars=where, mib=MEDIUM)
        return given, part, send(rest, ENDS_IN)

    def pass_on(c):
        w = widths[c]
        tile = tile_of(w, 1024)
        second = chain.call(
            add_part,
            (w // tile,),
            (firsts[c], parts[c]),
            [cols(2 * rows, tile, 0), cols(2 * rows, tile, 0, 1)],
            [shape((2 * rows, w), BF)],
            [cols(2 * rows, tile, 0)],
        )[0]
        seconds[c] = send(second, MIDDLE)

    def hand_out(c):
        w = widths[c]
        third_in = [cols(rows, w, 0, 1)] * 2
        if c + 1 == len(cuts):
            third = chain.call(
                add_part, (1,), (seconds[c], parts[c]), third_in, [shape((rows, w), BF)], [whole(rows, w)]
            )[0]
        else:
            v = widths[c + 1]
            third, second = chain.call(
                add_parts,
                (1,),
                (seconds[c], parts[c], firsts[c + 1], parts[c + 1]),
                [*third_in, whole(2 * rows, v), cols(2 * rows, v, 0, 1)],
                [shape((rows, w), BF), shape((2 * rows, v), BF)],
                [whole(rows, w), whole(2 * rows, v)],
            )
            seconds[c + 1] = send(second, MIDDLE)
        thirds[c] = send(third, PAIRS)

    def grads_of(c, g):
        start, w = group_cuts[g]
        tile = tile_of(math.gcd(start, w), 1024)
        at = start - cuts[c][0]
        own = chain.call(
            swiglu_grads,
            (w // tile,),
            (parts[c], seconds[c], thirds[c], saved_gate, saved_up),
            [cols(rows, tile, at)] * 3 + [cols(rows, tile, start)] * 2,
            [shape((2, rows, w), BF)],
            [pl.BlockSpec((2, rows, tile), lambda j: (0, 0, j))],
        )[0]
        return spread(own)

    def spread(own):
        return {"own": own, "pair": send(own, PAIRS), "near": send(own, MIDDLE)}

    def spread_near(x):
        (x["near"],) = chain.relay(x["near"])
        x["near_end"] = send(x["near"], OUTWARD)

    def spread_far(x):
        (x["pair"],) = chain.relay(x["pair"])
        x["far"] = send(x["pair"], MIDDLE)

    def spread_end(x, *others):
        x["far"], *others = chain.relay(x["far"], *others)
        x["far_end"] = send(x["far"], OUTWARD)
        return others

    def pieces(x):
        return [x[k] for k in ALL]

    def input_step(g, before, names):
        start, w = group_cuts[g]
        tile = tile_of(depth, 1024)
        wide = pl.BlockSpec((pl.Element(tile), pl.Element(w)), lambda j: (j * tile, start))
        count = len(names)
        height = rows * len([k for k in names if not k.endswith("_end")])
        across = cols(height, tile, 0)
        return chain.call(
            functools.partial(input_sums_first if before is None else input_sums_more, count),
            (depth // tile,),
            [*[groups[g][k] for k in names], w_gate, w_up] + ([] if before is None else [before]),
            [whole(2, rows, w)] * count + [wide, wide] + ([] if before is None else [across]),
            [shape((height, depth), F32)],
            [across],
            scratch=[pltpu.VMEM((2, height, w), BF)], mib=LARGE)[0]

    def far_more(x, cut, before):
        start, w = cut
        tile = tile_of(depth, LAST_TILE)
        wide = pl.BlockSpec((pl.Element(tile), pl.Element(w)), lambda j: (j * tile, start))
        return chain.call(
            functools.partial(input_sums_more, 2),
            (depth // tile,),
            [*x, w_gate, w_up, before],
            [whole(2, rows, w)] * 2 + [wide, wide, cols(rows, tile, 0, 3)],
            [shape((rows, depth), F32)],
            [cols(rows, tile, 0)],
            scratch=[pltpu.VMEM((2, rows, w), BF)],
            mib=LARGE,
        )[0]

    def far_last(x, cut, before, others):
        start, w = cut
        tile = tile_of(depth, LAST_TILE)
        wide = pl.BlockSpec((pl.Element(tile), pl.Element(w)), lambda j, *_: (j * tile, start))
        return chain.call(
            input_sums_last,
            (depth // tile,),
            [*x, w_gate, w_up, before, others],
            [whole(2, rows, w)] * 2 + [wide, wide, cols(rows, tile, 0), cols(3 * rows, tile, 0)],
            [shape((tokens // 2, depth), F32), shape((tokens // 2, depth), BF)],
            [cols(tokens // 2, tile, 0)] * 2,
            scalars=where,
            scratch=[pltpu.VMEM((2, rows, w), BF), pltpu.VMEM((tokens, tile), F32)],
            mib=LARGE,
        )

    def weights_step(x, cut, at, before):
        start, w = cut
        tile = tile_of(math.gcd(math.gcd(start, at), w), 1024)
        places = [at // tile if piece.shape[2] > w else 0 for piece in x]
        return chain.call(
            weight_grads,
            (w // tile,),
            (inputs, *x, *before),
            [whole(depth, tokens)]
            + [pl.BlockSpec((2, rows, tile), lambda j, p=p: (0, 0, p + j)) for p in places]
            + [ANY] * len(before),
            [shape((depth, ff), BF)] * 2,
            [cols(depth, tile, start)] * 2,
            aliases=[(7, 0), (8, 1)] if before else (),
            mib=LARGE,
        )

    def down_step():
        tile = tile_of(ff, 1024)
        return chain.call(
            down_grads,
            (ff // tile,),
            [grads, *pieces(h)],
            [whole(tokens, depth)] + [cols(rows, tile, 0)] * 6,
            [shape((ff, depth), BF)],
            [pl.BlockSpec((tile, depth), lambda j, *_: (j, 0))], mib=MEDIUM)[0]

    n = len(cuts)
    parts, firsts, seconds, thirds = ([None] * n for _ in range(4))
    out_grads = tok_swaps(out_grad)
    h = spread(Chain(jnp.zeros((8, 128), F32)).call(*hidden_args(), mib=WHOLE)[0])
    out_grads = tok_last(*out_grads)
    grads, parts[0], firsts[0] = partial(0)
    spread_near(h)
    spread_far(h)
    _, parts[1], firsts[1] = partial(1)
    pass_on(0)
    (h["near_end"],) = spread_end(h, h["near_end"])
    hand_out(0)
    (h["far_end"],) = chain.relay(h["far_end"])
    groups = [grads_of(0, 0)]
    down = down_step()
    hand_out(1)
    spread_far(groups[0])
    (thirds[1],) = chain.relay(thirds[1])
    spread_near(groups[0])
    groups.append(grads_of(1, 1))
    spread_end(groups[0])
    (groups[0]["near_end"],) = chain.relay(groups[0]["near_end"])
    spread_near(groups[1])
    spread_far(groups[1])
    (inputs_b,) = chain.relay(saved_input.astype(BF))
    in_raw = tok_last(*tok_swaps(inputs_b))
    inputs = chain.call(
        functools.partial(arrange, True),
        (1,),
        in_raw,
        [whole(rows, depth)] * 4,
        [shape((depth, tokens), BF)],
        [whole(depth, tokens)],
        scalars=where,
    )[0]
    (groups[0]["far_end"],) = chain.relay(groups[0]["far_end"])
    total = input_step(0, None, ALL)
    weights = weights_step(pieces(groups[0]), cuts[0], 0, ())
    second = ff - first
    part = second // 2
    low_cut, high_cut = (first, part), (first + part, part)
    low, high = chain.call(
        halves,
        (1,),
        (groups[1]["far"],),
        [whole(2, rows, second)],
        [shape((2, rows, part), BF)] * 2,
        [whole(2, rows, part)] * 2,
    )
    low, high = (low, send(low, OUTWARD)), (high, send(high, OUTWARD))
    early = [groups[1][k] for k in ALL[:4]]
    others = input_step(1, total, ALL[:4])
    total = far_more(low, low_cut, total)
    weights = weights_step([*early, *low], low_cut, 0, weights)
    mine, other = far_last(high, high_cut, total, others)
    got = lax.ppermute(other, "tok", CORE_SWAP)
    keep, *others = chain.call(
        split_again,
        (1,),
        (mine, got),
        [whole(tokens // 2, depth)] * 2,
        [shape((rows // 2, depth), F32), *[shape((rows // 2, depth), BF)] * 3],
        [whole(rows // 2, depth)] * 4,
        scalars=where,
    )
    got = (
        lax.ppermute(others[2], ("out", "tok"), XY_SWAP),
        lax.ppermute(others[0], "out", Y_SWAP),
        lax.ppermute(others[1], "tok", X_SWAP),
    )
    weights = weights_step([*early, *high], high_cut, part, weights)
    result = chain.call(
        add_last,
        (1,),
        (keep, got[1], got[2], got[0]),
        [whole(rows // 2, depth)] * 4,
        [shape((rows // 2, depth), BF)],
        [whole(rows // 2, depth)],
    )[0]
    return result, weights[0], weights[1], down


def any_line(saved_input, saved_gate, saved_up, out_grad, w_gate, w_up, w_down):
    inputs = lax.all_gather(saved_input.astype(BF), "tok", axis=0, tiled=True)
    grads = lax.all_gather(out_grad, "tok", axis=0, tiled=True)
    part = dot(grads, w_down, LAST)
    share = lax.psum_scatter(part, "inp", scatter_dimension=0, tiled=True)
    sig = jax.nn.sigmoid(saved_gate)
    gate = share * saved_up * sig * (1.0 + saved_gate * (1.0 - sig))
    up = share * saved_gate * sig
    hidden = saved_gate * sig * saved_up
    gate, up, hidden = (
        lax.all_gather(v.astype(BF), "inp", axis=0, tiled=True) for v in (gate, up, hidden)
    )
    total = dot(gate, w_gate, LAST) + dot(up, w_up, LAST)
    total = lax.psum_scatter(total, ("out", "tok"), scatter_dimension=0, tiled=True)
    return (
        total.astype(BF),
        dot(inputs, gate, LEAD).astype(BF),
        dot(inputs, up, LEAD).astype(BF),
        dot(hidden, grads, LEAD).astype(BF),
    )


def solution(mesh):
    sizes = dict(mesh.shape)
    placed = (
        P("tok", "inp"),
        P("inp", ("out", "tok")),
        P("inp", ("out", "tok")),
        P("tok", "inp"),
        P("inp", ("out", "tok")),
        P("inp", ("out", "tok")),
        P(("out", "tok"), "inp"),
    )

    def local(*args):
        rows, ff = args[1].shape
        fits = (sizes["inp"], sizes["out"], sizes["tok"]) == (4, 2, 4)
        if fits and rows % 32 == 0 and ff % 3584 == 0:
            return line_of_four(*args)
        return any_line(*args)

    return jax.shard_map(
        local,
        mesh=mesh,
        in_specs=placed,
        out_specs=(
            P(("out", "tok"), "inp"),
            P("inp", ("out", "tok")),
            P("inp", ("out", "tok")),
            P(("out", "tok"), "inp"),
        ),
        check_vma=False,
    )
```
